256 devices in a mesh: section: 8 (over x, y_lo), fsdp: 32 (over z, y_hi, core).
Axes of the slice: x: 4, y: 4 (y_hi: 2, y_lo: 2; y = y_hi * 2 + y_lo), z: 8, core: 2. Of those that a mesh axis runs over, the one named last changes fastest.
Arguments:
- upstream: bfloat16 [2, 4096, 4096], P(None, 'fsdp'), may hold values from -6 to 6
- saved_inputs: bfloat16 [8, 2, 2, 4096, 4096], P('section', None, None, 'fsdp'), may hold values from -6 to 6
- queries: bfloat16 [8, 2, 2, 4096, 512], P('section', None, None, 'fsdp'), may hold values from -24 to 24
- keys: bfloat16 [8, 2, 2, 4096, 512], P('section', None, None, 'fsdp'), may hold values from -24 to 24
- segments: int32 [2, 32, 128], P(None, 'fsdp'), may hold values from 0 to 3, never falling along the last dimension, each value on 1 to 64 neighbouring positions
- weights: bfloat16 [8, 2, 4096, 512], P('section', None, 'fsdp'), may hold values from -0.09375 to 0.09375
- gains: float32 [8, 2, 4096], P('section'), may hold values from 0.1 to 1.9
Outputs:
- boundary_grads: bfloat16 [8, 2, 4096, 4096], P('section', None, 'fsdp')
- weight_grad: float32 [8, 2, 4096, 512], P('section', None, 'fsdp')
The draws below stay inside these ranges and needn't reach their ends.
All inputs are finite; a program needn't handle non-finite values.
Results may differ from the reference program's by a relative error of at most 0.033.
Values may be sent and summed in bfloat16 or wider, within the bound.
No kernel may reach another device: no remote copies, remote signals or barrier semaphores. Data moves between devices by JAX's collectives and lax.ppermute only.
A program may use at most 128 MiB of HBM per device.

```python
import math
import jax
import jax.numpy as jnp
import numpy as np
from jax import lax

D = 4096
HEADS = 4
HEAD_DIM = 128
R = 512
TOK_DEV = 128
MB = 2
PACKS = 32
TOKENS = 4096
LAYERS = 16
N_SECTION = 8


def draw_queries(key, part):
    key = jax.random.fold_in(key, 11)
    key_base = jax.random.fold_in(key, 0)
    shape = (N_SECTION, 2, MB, TOKENS, HEADS, HEAD_DIM)
    base = jnp.clip(jax.random.normal(key_base, shape, jnp.float32), -4.0, 4.0)
    return base.reshape(N_SECTION, 2, MB, TOKENS, HEADS * HEAD_DIM).astype(jnp.bfloat16)


def draw_keys(key, part):
    key = jax.random.fold_in(key, 13)
    key_base = jax.random.fold_in(key, 0)
    shape = (N_SECTION, 2, MB, TOKENS, HEADS, HEAD_DIM)
    base = jnp.clip(jax.random.normal(key_base, shape, jnp.float32), -4.0, 4.0)
    return base.reshape(N_SECTION, 2, MB, TOKENS, HEADS * HEAD_DIM).astype(jnp.bfloat16)


def spiked(entries, own_key, source, target, parts, factor):
    def block_of(axis_at):
        return (jnp.arange(entries.shape[axis_at]) // (entries.shape[axis_at] // parts)).reshape((-1,) + (1,) * (entries.ndim - 1 - axis_at))

    one_side = jax.random.permutation(own_key, parts)[block_of(target)]
    second = (block_of(target) + parts // 2) % parts
    return jnp.where((block_of(source) == one_side) | (block_of(source) == second), factor * entries, entries)


def levels(own_key, dims, shards, smallest, largest):
    level, own = 1.0, jax.random.fold_in(own_key, 6)
    for dim, blocks in shards:
        heights = jnp.exp(jax.random.uniform(jax.random.fold_in(own, dim), (blocks,), jnp.float32, smallest / len(shards), largest / len(shards)))
        level = level * jnp.repeat(heights, dims[dim] // blocks).reshape([-1 if axis == dim else 1 for axis in range(len(dims))])
    return level


def split_up(number_of, total, bound, lean):
    weights = [(1 << 20) // math.isqrt(rank ** lean) + 1 for rank in range(2, number_of + 1)]
    surplus, counts = total - bound - (number_of - 1), [1] * (number_of - 1)
    while surplus > 0:
        candidates = [i for i in range(number_of - 1) if counts[i] < bound]
        pool, left = sum([weights[i] for i in candidates]), surplus
        for i in candidates:
            extra = min(bound - counts[i], max(1, left * weights[i] // pool), surplus)
            counts[i] = counts[i] + extra
            surplus = surplus - extra
    return np.array([bound] + counts)


def ragged_sizes(rng, number_of, total, bound, lean):
    if number_of == 2:
        one = jax.random.randint(rng, (), max(1, total - bound), min(bound, total - 1) + 1)
        return jnp.stack([one, total - one])
    tallies = jnp.asarray(split_up(number_of, total, bound, lean), jnp.int32)
    pairs = (number_of - 1) // 2
    giver, sink = tallies[1:1 + 2 * pairs:2], tallies[2:2 + 2 * pairs:2]
    slack = jnp.minimum(giver - 1, bound - sink)
    shifted = jax.random.randint(jax.random.fold_in(rng, 1), (pairs,), 0, 1 << 20) % (slack + 1)
    tallies = tallies.at[1:1 + 2 * pairs:2].set(giver - shifted).at[2:2 + 2 * pairs:2].set(sink + shifted)
    return tallies[jax.random.permutation(jax.random.fold_in(rng, 2), number_of)]


def gaussian(rng, extent, spread, reach, cuts=(), held_as=jnp.bfloat16):
    values = spread * jax.random.normal(rng, extent, jnp.float32)
    if cuts:
        values = values * levels(rng, extent, cuts, -0.22, 0.18)
    return jnp.clip(values, -reach, reach).astype(held_as)


def heavy_noise(stream_key, dims, scale, limit, cuts, heavy, held_as=jnp.bfloat16):
    result = scale * jax.random.normal(stream_key, dims, jnp.float32)
    if cuts:
        result = result * levels(stream_key, dims, cuts, -0.22, 0.18)
    return jnp.clip(spiked(result, jax.random.fold_in(stream_key, 3), *heavy), -limit, limit).astype(held_as)


def setup_inputs(seed: int = 0) -> dict:
    splits = jax.random.split(jax.random.key(seed), 8)
    upstream = heavy_noise(splits[0], (MB, TOKENS, D), 1.0, 6.0, ((1, 32),), (1, 2, 32, 2.75))
    saved_inputs = gaussian(splits[1], (N_SECTION, 2, MB, TOKENS, D), 1.0, 6.0, ((0, 8), (3, 32)))
    queries = draw_queries(jax.random.fold_in(splits[7], 71), 0)
    keys = draw_keys(jax.random.fold_in(splits[7], 71), 0)
    segments = jax.vmap(lambda own: jnp.searchsorted(jnp.cumsum(ragged_sizes(own, 4, TOK_DEV, TOK_DEV // 2, 1)), jnp.arange(TOK_DEV), side="right"))(jax.random.split(splits[4], MB * PACKS)).reshape((MB, PACKS, TOK_DEV)).astype(jnp.int32)
    weights = gaussian(splits[5], (N_SECTION, 2, D, R), D ** -0.5, 0.09375, ((0, 8), (2, 32)))
    gains = jnp.clip(1.0 + 0.18 * jax.random.normal(splits[6], (N_SECTION, 2, D), jnp.float32), 0.1, 1.9)
    return dict(upstream=upstream, saved_inputs=saved_inputs, queries=queries, keys=keys, segments=segments, weights=weights, gains=gains)


EPS = 1e-05

def attention_weights(queries, keys, segment):
    length = queries.shape[0]
    q_heads = queries.reshape(length, HEADS, HEAD_DIM).astype(jnp.float32)
    k_heads = keys.reshape(length, HEADS, HEAD_DIM).astype(jnp.float32)
    scores = jnp.einsum('tad,sad->ats', q_heads, k_heads) * (1.0 / math.sqrt(HEAD_DIM))
    position = jnp.arange(length)
    allowed = (position[:, None] >= position[None, :]) & (segment[:, None] == segment[None, :])
    scores = jnp.where(allowed[None], scores, -1e+30)
    peak = lax.optimization_barrier(jnp.max(scores, -1, keepdims=True))
    expo = jnp.where(allowed[None], jnp.exp(scores - peak), 0.0)
    return (expo / lax.optimization_barrier(jnp.sum(expo, -1, keepdims=True))).astype(jnp.bfloat16)

def pack_backward(upstream_gradient, xin, queries, keys, segment, weight, norm_gain_vector):
    length = upstream_gradient.shape[0]
    gathered_input = xin.astype(jnp.float32)
    inverse_norm_scale = lax.rsqrt(lax.optimization_barrier(jnp.mean(gathered_input * gathered_input, -1, keepdims=True)) + EPS)
    standardized_input = gathered_input * inverse_norm_scale
    normalized_rows = (standardized_input * norm_gain_vector).astype(jnp.bfloat16)
    probs = attention_weights(queries, keys, segment).astype(jnp.float32)
    values = jnp.dot(normalized_rows, weight, preferred_element_type=jnp.float32).astype(jnp.bfloat16)
    value_heads = values.reshape(length, HEADS, HEAD_DIM).astype(jnp.float32)
    mixed = jnp.einsum('ats,sad->tad', probs, value_heads).reshape(length, R).astype(jnp.bfloat16)
    dmix = jnp.dot(upstream_gradient, weight, preferred_element_type=jnp.float32).astype(jnp.bfloat16)
    dmix_heads = dmix.reshape(length, HEADS, HEAD_DIM).astype(jnp.float32)
    dvalues = jnp.einsum('ats,tad->sad', probs, dmix_heads).reshape(length, R).astype(jnp.bfloat16)
    dnormed = lax.dot_general(dvalues, weight, (((1,), (1,)), ((), ())), preferred_element_type=jnp.float32)
    centered_input_gradient = dnormed * norm_gain_vector
    backward_output = upstream_gradient.astype(jnp.float32) + inverse_norm_scale * (centered_input_gradient - standardized_input * lax.optimization_barrier(jnp.mean(centered_input_gradient * standardized_input, -1, keepdims=True)))
    return (backward_output.astype(jnp.bfloat16), normalized_rows, mixed, dvalues)

def pack_major(array):
    width = array.shape[-1]
    shaped = array.reshape(MB, PACKS, TOK_DEV, width)
    return jnp.transpose(shaped, (1, 0, 2, 3)).reshape(PACKS, MB * TOK_DEV, width)

def add_pack(total, item):
    grad_rows, normed_rows, mixed_rows, dvalue_rows = item
    contract = (((0,), (0,)), ((), ()))
    term = lax.dot_general(grad_rows, mixed_rows, contract, preferred_element_type=jnp.float32)
    term = term + lax.dot_general(normed_rows, dvalue_rows, contract, preferred_element_type=jnp.float32)
    rounded = lax.optimization_barrier(term.astype(jnp.bfloat16)).astype(jnp.float32)
    return (total + rounded, None)

def reference(upstream, saved_inputs, queries, keys, segments, weights, gains):
    seg_rows = segments.reshape(MB * PACKS, TOK_DEV)
    upstream_gradient = upstream.reshape(MB * PACKS, TOK_DEV, D)
    run_packs = jax.vmap(pack_backward, in_axes=(0, 0, 0, 0, 0, None, None))
    boundary = [None] * N_SECTION
    grads_of = [[None, None] for section in range(N_SECTION)]
    for layer in reversed(range(LAYERS)):
        section, group = (layer // 2, layer % 2)
        xin = saved_inputs[section, group].reshape(MB * PACKS, TOK_DEV, D)
        q_rows = queries[section, group].reshape(MB * PACKS, TOK_DEV, R)
        k_rows = keys[section, group].reshape(MB * PACKS, TOK_DEV, R)
        backward_output, normalized_rows, mixed, dvalues = run_packs(upstream_gradient, xin, q_rows, k_rows, seg_rows, weights[section, group], gains[section, group])
        items = (pack_major(upstream_gradient), pack_major(normalized_rows), pack_major(mixed), pack_major(dvalues))
        total, unused = lax.scan(add_pack, jnp.zeros((D, R), jnp.float32), items)
        grads_of[section][group] = total / PACKS
        upstream_gradient = backward_output
        if group == 0:
            boundary[section] = backward_output.reshape(MB, TOKENS, D)
    weight_grad = jnp.stack([jnp.stack(pair, 0) for pair in grads_of], 0)
    return (jnp.stack(boundary, 0), weight_grad)
```

```python
import functools
import math

import jax
import jax.numpy as jnp
from jax import lax
from jax.experimental import pallas as pl
from jax.experimental.pallas import tpu as pltpu
from jax.sharding import PartitionSpec as P

HEADS = 4
HEAD_DIM = 128
EPS = 1e-05
CHUNK = 512
VMEM_LIMIT = 48 * 1024 * 1024


def pre_kernel(x_ref, q_ref, k_ref, seg_row_ref, seg_col_ref, rstd_ref, probs_ref):
    length, width = x_ref.shape[2:]
    total = jnp.zeros((length, 1), jnp.float32)
    for at in range(0, width, CHUNK):
        part = x_ref[0, 0, :, at : at + CHUNK].astype(jnp.float32)
        total += jnp.sum(part * part, -1, keepdims=True)
    rstd = lax.rsqrt(total / width + EPS)
    rstd_ref[0, 0] = jnp.broadcast_to(rstd, (length, 128))
    rows = lax.broadcasted_iota(jnp.int32, (length, length), 0)
    columns = lax.broadcasted_iota(jnp.int32, (length, length), 1)
    allowed = (rows >= columns) & (seg_col_ref[0] == seg_row_ref[0])
    for head in range(HEADS):
        own = slice(head * HEAD_DIM, (head + 1) * HEAD_DIM)
        scores = lax.dot_general(
            q_ref[0, 0, :, own],
            k_ref[0, 0, :, own],
            (((1,), (1,)), ((), ())),
            preferred_element_type=jnp.float32,
        ) * (1.0 / math.sqrt(HEAD_DIM))
        scores = jnp.where(allowed, scores, -1e30)
        peak = jnp.max(scores, -1, keepdims=True)
        expo = jnp.where(allowed, jnp.exp(scores - peak), 0.0)
        probs = expo / jnp.sum(expo, -1, keepdims=True)
        probs_ref[0, 0, head] = probs.astype(jnp.bfloat16)


def value_kernel(x_ref, rstd_ref, gain_ref, w_ref, probs_ref, vals_ref, mixed_ref):
    batches, length, width = x_ref.shape[1:]
    rank = w_ref.shape[2]
    acc = jnp.zeros((batches * length, rank), jnp.float32)
    for at in range(0, width, CHUNK):
        gain = gain_ref[0, :, at : at + CHUNK]
        normed = [
            (x_ref[0, m, :, at : at + CHUNK].astype(jnp.float32) * rstd_ref[0, m, :, 0:1] * gain)
            .astype(jnp.bfloat16)
            for m in range(batches)
        ]
        acc += jnp.dot(
            jnp.concatenate(normed, 0),
            w_ref[0, at : at + CHUNK, :],
            preferred_element_type=jnp.float32,
        )
    for m in range(batches):
        part = acc[m * length : (m + 1) * length]
        vals_ref[0, m] = part
        values = part.astype(jnp.bfloat16)
        for head in range(HEADS):
            own = slice(head * HEAD_DIM, (head + 1) * HEAD_DIM)
            mixed_ref[0, m, :, own] = jnp.dot(
                probs_ref[0, m, head], values[:, own], preferred_element_type=jnp.float32
            ).astype(jnp.bfloat16)


def tick_kernel(
    place_ref, incoming, upstream, saved, weight, gains, probs, vals, rstd,
    grads_in, dvs_in, boundary_in,
    out, grads, dvs, boundary,
    g_buf, x_buf, w_buf, gain_buf, p_buf, v_buf, r_buf, dv_buf, sems,
):
    del grads_in, dvs_in, boundary_in
    micro, top = place_ref[0], place_ref[1]
    batches = upstream.shape[0]
    width = incoming.shape[1]
    rank = weight.shape[2]
    count = width // CHUNK

    @pl.when((micro >= 0) & (micro < batches))
    def _():
        used = [0]

        def copy(source, target):
            made = pltpu.make_async_copy(source, target, sems.at[used[0]])
            used[0] += 1
            return made

        from_top = copy(upstream.at[micro], g_buf.at[0])
        from_above = pltpu.make_async_copy(incoming, g_buf.at[0], sems.at[used[0] - 1])

        @pl.when(top == 1)
        def _():
            from_top.start()

        @pl.when(top == 0)
        def _():
            from_above.start()

        load_w, load_x, load_p, load_v, load_r = ({}, {}, {}, {}, {})
        load_gain = copy(gains, gain_buf)
        for layer in (1, 0):
            for c in range(count):
                rows = pl.ds(c * CHUNK, CHUNK)
                load_w[layer, c] = copy(weight.at[layer, rows], w_buf.at[layer, rows])
            load_p[layer] = copy(probs.at[layer, micro], p_buf.at[layer])
            load_v[layer] = copy(vals.at[layer, micro], v_buf.at[layer])
            load_r[layer] = copy(rstd.at[layer, micro], r_buf.at[layer])
            load_x[layer] = copy(saved.at[layer, micro], x_buf.at[layer])
        for layer in (1, 0):
            for c in range(count):
                load_w[layer, c].start()
                if layer == 1 and c == 0:
                    load_gain.start()
            load_p[layer].start()
            load_v[layer].start()
            load_r[layer].start()
            load_x[layer].start()

        from_top.wait()
        stores = [copy(g_buf.at[0], grads.at[1, micro])]
        stores[0].start()
        acc = None
        for c in range(count):
            load_w[1, c].wait()
            rows = slice(c * CHUNK, (c + 1) * CHUNK)
            term = jnp.dot(
                g_buf[0, :, rows], w_buf[1, rows, :], preferred_element_type=jnp.float32
            )
            acc = term if acc is None else acc + term
        load_gain.wait()
        for step, layer in enumerate((1, 0)):
            dmix = acc.astype(jnp.bfloat16)
            load_p[layer].wait()
            for head in range(HEADS):
                own = slice(head * HEAD_DIM, (head + 1) * HEAD_DIM)
                dv_buf[layer, :, own] = lax.dot_general(
                    p_buf[layer, head],
                    dmix[:, own],
                    (((0,), (0,)), ((), ())),
                    preferred_element_type=jnp.float32,
                ).astype(jnp.bfloat16)
            stores.append(copy(dv_buf.at[layer], dvs.at[layer, micro]))
            stores[-1].start()
            dv = dv_buf[layer]
            load_v[layer].wait()
            load_r[layer].wait()
            scale = r_buf[layer, :, 0:1]
            mean = jnp.sum(dv.astype(jnp.float32) * v_buf[layer], -1, keepdims=True) / width
            pull = scale * scale * mean
            load_x[layer].wait()
            acc = None
            for c in range(count):
                rows = slice(c * CHUNK, (c + 1) * CHUNK)
                dnormed = lax.dot_general(
                    dv, w_buf[layer, rows, :], (((1,), (1,)), ((), ())),
                    preferred_element_type=jnp.float32,
                )
                lower = (
                    g_buf[step, :, rows].astype(jnp.float32)
                    + scale * (dnormed * gain_buf[layer : layer + 1, rows])
                    - x_buf[layer, :, rows].astype(jnp.float32) * pull
                ).astype(jnp.bfloat16)
                g_buf[step + 1, :, rows] = lower
                if layer == 1:
                    load_w[0, c].wait()
                    term = jnp.dot(
                        lower, w_buf[0, rows, :], preferred_element_type=jnp.float32
                    )
                    acc = term if acc is None else acc + term
            if layer == 1:
                stores.append(copy(g_buf.at[1], grads.at[0, micro]))
                stores[-1].start()
        stores.append(copy(g_buf.at[2], out))
        stores[-1].start()
        stores.append(copy(g_buf.at[2], boundary.at[micro]))
        stores[-1].start()
        for store in stores:
            store.wait()


def weight_kernel(g_ref, x_ref, rstd_ref, gain_ref, mixed_ref, dv_ref, out_ref):
    batches = g_ref.shape[1]
    left, right = ([], [])
    for m in range(batches):
        left.append(g_ref[0, m])
        right.append(mixed_ref[0, m])
    for m in range(batches):
        left.append(
            (x_ref[0, m].astype(jnp.float32) * rstd_ref[0, m, :, 0:1] * gain_ref[0])
            .astype(jnp.bfloat16)
        )
        right.append(dv_ref[0, m])
    out_ref[0] = lax.dot_general(
        jnp.concatenate(left, 0),
        jnp.concatenate(right, 0),
        (((0,), (0,)), ((), ())),
        preferred_element_type=jnp.float32,
    ).astype(jnp.bfloat16)


def params(**more):
    return pltpu.CompilerParams(vmem_limit_bytes=VMEM_LIMIT, **more)


def body(upstream, saved_inputs, queries, keys, segments, weights, gains):
    sections = lax.axis_size("section")
    section_index = lax.axis_index("section")
    shards = lax.axis_size("fsdp")
    batches, length, width = upstream.shape
    rank = weights.shape[3]
    saved = saved_inputs[0]
    seg_row = segments
    seg_col = jnp.transpose(segments, (0, 2, 1))
    gain_rows = gains[0][:, None, :]
    bf16, f32 = (jnp.bfloat16, jnp.float32)
    shape = jax.ShapeDtypeStruct
    any_spec = pl.BlockSpec(memory_space=pl.ANY)

    full_weight = lax.all_gather(weights, "fsdp", axis=2, tiled=True)[0]

    pair = lambda *tail: pl.BlockSpec((1, 1) + tail, lambda l, m: (l, m) + (0,) * len(tail))
    rstd, probs = pl.pallas_call(
        pre_kernel,
        grid=(2, batches),
        in_specs=[
            pair(length, width),
            pair(length, rank),
            pair(length, rank),
            pl.BlockSpec((1, 1, length), lambda l, m: (m, 0, 0)),
            pl.BlockSpec((1, length, 1), lambda l, m: (m, 0, 0)),
        ],
        out_specs=[pair(length, 128), pair(HEADS, length, length)],
        out_shape=[
            shape((2, batches, length, 128), f32),
            shape((2, batches, HEADS, length, length), bf16),
        ],
        compiler_params=params(),
        name="rows_alone",
    )(saved, queries[0], keys[0], seg_row, seg_col)

    each = lambda *tail: pl.BlockSpec((1,) + tail, lambda l: (l,) + (0,) * len(tail))
    vals, mixed = pl.pallas_call(
        value_kernel,
        grid=(2,),
        in_specs=[
            each(batches, length, width),
            each(batches, length, 128),
            each(1, width),
            each(width, rank),
            each(batches, HEADS, length, length),
        ],
        out_specs=[each(batches, length, rank), each(batches, length, rank)],
        out_shape=[
            shape((2, batches, length, rank), f32),
            shape((2, batches, length, rank), bf16),
        ],
        compiler_params=params(),
        name="values",
    )(saved, rstd, gain_rows, full_weight, probs)

    tick = pl.pallas_call(
        tick_kernel,
        in_specs=[pl.BlockSpec(memory_space=pltpu.SMEM)] + [any_spec] * 11,
        out_specs=[any_spec] * 4,
        out_shape=[
            shape((length, width), bf16),
            shape((2, batches, length, width), bf16),
            shape((2, batches, length, rank), bf16),
            shape((batches, length, width), bf16),
        ],
        input_output_aliases={9: 1, 10: 2, 11: 3},
        scratch_shapes=[
            pltpu.VMEM((3, length, width), bf16),
            pltpu.VMEM((2, length, width), bf16),
            pltpu.VMEM((2, width, rank), bf16),
            pltpu.VMEM((2, width), f32),
            pltpu.VMEM((2, HEADS, length, length), bf16),
            pltpu.VMEM((2, length, rank), f32),
            pltpu.VMEM((2, length, 128), f32),
            pltpu.VMEM((2, length, rank), bf16),
            pltpu.SemaphoreType.DMA((40,)),
        ],
        compiler_params=params(),
        name="section",
    )

    incoming = upstream[0]
    grads = jnp.zeros((2, batches, length, width), bf16)
    dvs = jnp.zeros((2, batches, length, rank), bf16)
    boundary = jnp.zeros((batches, length, width), bf16)
    top = (section_index == sections - 1).astype(jnp.int32)
    for step in range(sections + batches - 1):
        micro = step - (sections - 1 - section_index)
        place = jnp.stack([micro.astype(jnp.int32), top])
        out, grads, dvs, boundary = tick(
            place, incoming, upstream, saved, full_weight, gains[0], probs, vals, rstd,
            grads, dvs, boundary,
        )
        if step < sections + batches - 2:
            senders = [sections - 1 - step + m for m in range(batches)]
            incoming = lax.ppermute(
                out, "section", [(s, s - 1) for s in senders if 1 <= s < sections]
            )

    both = lambda *tail: pl.BlockSpec((1, batches) + tail, lambda l, c: (l, 0) + (0,) * len(tail))
    cols = lambda: pl.BlockSpec((1, batches, length, CHUNK), lambda l, c: (l, 0, 0, c))
    partial = pl.pallas_call(
        weight_kernel,
        grid=(2, width // CHUNK),
        in_specs=[
            cols(),
            cols(),
            both(length, 128),
            pl.BlockSpec((1, 1, CHUNK), lambda l, c: (l, 0, c)),
            both(length, rank),
            both(length, rank),
        ],
        out_specs=pl.BlockSpec((1, CHUNK, rank), lambda l, c: (l, c, 0)),
        out_shape=shape((2, width, rank), bf16),
        compiler_params=params(),
        name="partial",
    )(grads, saved, rstd, gain_rows, mixed, dvs)
    summed = lax.psum_scatter(partial, "fsdp", scatter_dimension=1, tiled=True)
    weight_grad = (summed.astype(f32) / shards)[None]
    return (boundary[None], weight_grad)


def solution(mesh):
    return jax.shard_map(
        body,
        mesh=mesh,
        in_specs=(
            P(None, "fsdp", None),
            P("section", None, None, "fsdp", None),
            P("section", None, None, "fsdp", None),
            P("section", None, None, "fsdp", None),
            P(None, "fsdp", None),
            P("section", None, "fsdp", None),
            P("section", None, None),
        ),
        out_specs=(P("section", None, "fsdp", None), P("section", None, "fsdp", None)),
        check_vma=False,
    )
```

```python
import functools
import math

import jax
import jax.numpy as jnp
from jax import lax
from jax.experimental import pallas as pl
from jax.experimental.pallas import tpu as pltpu
from jax.sharding import PartitionSpec as P

HEADS = 4
HEAD_DIM = 128
EPS = 1e-05
CHUNK = 512
BLOCKS = 16
RING = 7
VMEM_LIMIT = 20 * 1024 * 1024
VMEM_VALUES = 56 * 1024 * 1024
VMEM_ALL = 62 * 1024 * 1024


def pre_kernel(x_ref, q_ref, k_ref, seg_row_ref, seg_col_ref, rstd_ref, probs_ref):
    length, width = x_ref.shape[2:]
    total = jnp.zeros((length, 1), jnp.float32)
    for at in range(0, width, CHUNK):
        part = x_ref[0, 0, :, at : at + CHUNK].astype(jnp.float32)
        total += jnp.sum(part * part, -1, keepdims=True)
    rstd = lax.rsqrt(total / width + EPS)
    rstd_ref[0, 0] = jnp.broadcast_to(rstd, (length, 128))
    rows = lax.broadcasted_iota(jnp.int32, (length, length), 0)
    columns = lax.broadcasted_iota(jnp.int32, (length, length), 1)
    allowed = (rows >= columns) & (seg_col_ref[0] == seg_row_ref[0])
    for head in range(HEADS):
        own = slice(head * HEAD_DIM, (head + 1) * HEAD_DIM)
        scores = lax.dot_general(
            q_ref[0, 0, :, own],
            k_ref[0, 0, :, own],
            (((1,), (1,)), ((), ())),
            preferred_element_type=jnp.float32,
        ) * (1.0 / math.sqrt(HEAD_DIM))
        scores = jnp.where(allowed, scores, -1e30)
        peak = jnp.max(scores, -1, keepdims=True)
        expo = jnp.where(allowed, jnp.exp(scores - peak), 0.0)
        probs = expo / jnp.sum(expo, -1, keepdims=True)
        probs_ref[0, 0, head] = probs.astype(jnp.bfloat16)


def value_kernel(place_ref, *refs):
    blocks, refs = refs[:BLOCKS], refs[BLOCKS:]
    saved, rstd, gains, probs, weight, vals, mixed, _, _, _, _, w_buf, x_buf, sems, x_sem, out_sem = refs
    batches, length, width = saved.shape[1:]
    rank = w_buf.shape[2]
    x_copies = [
        pltpu.make_async_copy(saved.at[layer], x_buf.at[layer], x_sem.at[layer]) for layer in (0, 1)
    ]
    loads = [[], []]
    rows = blocks[0].shape[2]
    for layer in (1, 0):
        for at, block in enumerate(blocks):
            for slot in (0, 1):
                start = pl.multiple_of(place_ref[2 * at + slot], rows)
                made = pltpu.make_async_copy(
                    block.at[slot, layer],
                    w_buf.at[layer, pl.ds(start, rows)],
                    sems.at[layer, 2 * at + slot],
                )
                made.start()
                loads[layer].append(made)
        x_copies[layer].start()
    stores = []
    for layer in (1, 0):
        for made in loads[layer]:
            made.wait()
        store = pltpu.make_async_copy(w_buf.at[layer], weight.at[layer], out_sem.at[layer])
        store.start()
        stores.append(store)
        x_copies[layer].wait()
        acc = jnp.zeros((batches * length, rank), jnp.float32)
        for at in range(0, width, CHUNK):
            cut = slice(at, at + CHUNK)
            gain = gains[layer : layer + 1, cut]
            normed = [
                (x_buf[layer, m, :, cut].astype(jnp.float32) * rstd[layer, m, :, 0:1] * gain)
                .astype(jnp.bfloat16)
                for m in range(batches)
            ]
            acc += jnp.dot(
                jnp.concatenate(normed, 0),
                w_buf[layer, cut, :],
                preferred_element_type=jnp.float32,
            )
        for m in range(batches):
            part = acc[m * length : (m + 1) * length]
            vals[layer, m] = part
            values = part.astype(jnp.bfloat16)
            for head in range(HEADS):
                own = slice(head * HEAD_DIM, (head + 1) * HEAD_DIM)
                mixed[layer, m, :, own] = jnp.dot(
                    probs[layer, m, head], values[:, own], preferred_element_type=jnp.float32
                ).astype(jnp.bfloat16)
    for store in stores:
        store.wait()


def tick_kernel(
    place_ref, incoming, upstream, saved, weight, gains, probs, vals, rstd,
    grads_in, dvs_in, boundary_in,
    out, grads, dvs, boundary,
    g_buf, x_buf, w_buf, gain_buf, p_buf, v_buf, r_buf, dv_buf, sems,
):
    del grads_in, dvs_in, boundary_in
    micro, top = place_ref[0], place_ref[1]
    batches = upstream.shape[0]
    width = incoming.shape[1]
    rank = weight.shape[2]
    count = width // CHUNK

    @pl.when((micro >= 0) & (micro < batches))
    def _():
        used = [0]

        def copy(source, target):
            made = pltpu.make_async_copy(source, target, sems.at[used[0]])
            used[0] += 1
            return made

        from_top = copy(upstream.at[micro], g_buf.at[0])
        from_above = pltpu.make_async_copy(incoming, g_buf.at[0], sems.at[used[0] - 1])

        @pl.when(top == 1)
        def _():
            from_top.start()

        @pl.when(top == 0)
        def _():
            from_above.start()

        load_w, load_x, load_p, load_v, load_r = ({}, {}, {}, {}, {})
        load_gain = copy(gains, gain_buf)
        for layer in (1, 0):
            for c in range(count):
                rows = pl.ds(c * CHUNK, CHUNK)
                load_w[layer, c] = copy(weight.at[layer, rows], w_buf.at[layer, rows])
            load_p[layer] = copy(probs.at[layer, micro], p_buf.at[layer])
            load_v[layer] = copy(vals.at[layer, micro], v_buf.at[layer])
            load_r[layer] = copy(rstd.at[layer, micro], r_buf.at[layer])
            load_x[layer] = copy(saved.at[layer, micro], x_buf.at[layer])
        for c in range(count):
            load_w[1, c].start()
        for made in (load_p[1], load_v[1], load_r[1], load_gain, load_x[1]):
            made.start()
        for c in range(count):
            load_w[0, c].start()
        for made in (load_p[0], load_v[0], load_r[0], load_x[0]):
            made.start()

        from_top.wait()
        acc = None
        for c in range(count):
            load_w[1, c].wait()
            rows = slice(c * CHUNK, (c + 1) * CHUNK)
            term = jnp.dot(
                g_buf[0, :, rows], w_buf[1, rows, :], preferred_element_type=jnp.float32
            )
            acc = term if acc is None else acc + term
        stores = [copy(g_buf.at[0], grads.at[1, micro])]
        stores[0].start()
        load_gain.wait()
        for step, layer in enumerate((1, 0)):
            dmix = acc.astype(jnp.bfloat16)
            load_p[layer].wait()
            for head in range(HEADS):
                own = slice(head * HEAD_DIM, (head + 1) * HEAD_DIM)
                dv_buf[layer, :, own] = lax.dot_general(
                    p_buf[layer, head],
                    dmix[:, own],
                    (((0,), (0,)), ((), ())),
                    preferred_element_type=jnp.float32,
                ).astype(jnp.bfloat16)
            stores.append(copy(dv_buf.at[layer], dvs.at[layer, micro]))
            stores[-1].start()
            dv = dv_buf[layer]
            load_v[layer].wait()
            load_r[layer].wait()
            scale = r_buf[layer, :, 0:1]
            mean = jnp.sum(dv.astype(jnp.float32) * v_buf[layer], -1, keepdims=True) / width
            pull = scale * scale * mean
            load_x[layer].wait()
            acc = None
            for c in range(count):
                rows = slice(c * CHUNK, (c + 1) * CHUNK)
                dnormed = lax.dot_general(
                    dv, w_buf[layer, rows, :], (((1,), (1,)), ((), ())),
                    preferred_element_type=jnp.float32,
                )
                lower = (
                    g_buf[step, :, rows].astype(jnp.float32)
                    + scale * (dnormed * gain_buf[layer : layer + 1, rows])
                    - x_buf[layer, :, rows].astype(jnp.float32) * pull
                ).astype(jnp.bfloat16)
                g_buf[step + 1, :, rows] = lower
                if layer == 1:
                    load_w[0, c].wait()
                    term = jnp.dot(
                        lower, w_buf[0, rows, :], preferred_element_type=jnp.float32
                    )
                    acc = term if acc is None else acc + term
            if layer == 1:
                stores.append(copy(g_buf.at[1], grads.at[0, micro]))
                stores[-1].start()
        stores.append(copy(g_buf.at[2], out))
        stores[-1].start()
        stores.append(copy(g_buf.at[2], boundary.at[micro]))
        stores[-1].start()
        for store in stores:
            store.wait()


def transpose_kernel(mixed_ref, dv_ref, right_ref):
    batches, length = mixed_ref.shape[1:3]
    rows = batches * length
    for layer in (0, 1):
        for m in range(batches):
            at = m * length
            right_ref[layer, :, at : at + length] = mixed_ref[layer, m].T
            right_ref[layer, :, rows + at : rows + at + length] = dv_ref[layer, m].T


def weight_kernel(split, tiles, place_ref, g_ref, x_ref, rstd_ref, gain_ref, right_ref, *refs):
    first_out, second_out, buf, sems = refs
    batches, length = g_ref.shape[1:3]
    wide = 2 * length

    def store(tile, slot, target, at):
        return pltpu.make_async_copy(buf.at[slot], target.at[at], sems.at[slot])

    def step(tile, carry):
        slot = lax.rem(tile, 2)
        start = pl.multiple_of(place_ref[tile] * wide, wide)
        cut = pl.ds(start, wide)

        @pl.when(tile >= 2)
        def _():
            store(tile, slot, first_out, 0).wait()

        for layer in (0, 1):
            left = [g_ref[layer, m, :, cut] for m in range(batches)]
            left += [
                (
                    x_ref[layer, m, :, cut].astype(jnp.float32)
                    * rstd_ref[layer, m, :, 0:1]
                    * gain_ref[layer : layer + 1, cut]
                ).astype(jnp.bfloat16)
                for m in range(batches)
            ]
            result = jnp.dot(
                right_ref[layer], jnp.concatenate(left, 0), preferred_element_type=jnp.float32
            ).astype(jnp.bfloat16)
            turned = place_ref[tiles + tile]
            buf[slot, turned, layer] = result[:, :length]
            buf[slot, 1 - turned, layer] = result[:, length:]

        @pl.when(tile < split)
        def _():
            store(tile, slot, first_out, jnp.minimum(tile, split - 1)).start()

        @pl.when(tile >= split)
        def _():
            store(tile, slot, second_out, jnp.maximum(tile - split, 0)).start()

        return carry

    lax.fori_loop(0, tiles, step, 0)
    for tile in (tiles - 2, tiles - 1):
        store(tile, tile % 2, first_out, 0).wait()


def params(limit=VMEM_LIMIT):
    return pltpu.CompilerParams(vmem_limit_bytes=limit)


def other_core(value, shards):
    return lax.ppermute(value, "fsdp", [(d, d ^ 1) for d in range(shards)])


def other_y(value, shards):
    return lax.ppermute(value, "fsdp", [(d, d ^ 2) for d in range(shards)])


def along_z(value, shards):
    return lax.ppermute(
        value, "fsdp", [(d, (d + (4 if d % 2 == 0 else shards - 4)) % shards) for d in range(shards)]
    )


def gather_blocks(own_rows, shards, core, early):
    near = jnp.stack([own_rows, other_core(own_rows, shards)])
    rows_near = [near]
    far_rows = other_y(own_rows, shards)
    near = along_z(near, shards)
    near, far_rows = lax.optimization_barrier((near, far_rows))
    rows_near += [near, other_core(near, shards)]
    far = jnp.stack([far_rows, other_core(far_rows, shards)])
    rows_far = [far]
    for k in (1, 2, 3):
        if k == 2:
            far, early = lax.optimization_barrier((far, early))
        if k > 1:
            near = along_z(near, shards)
            rows_near += [near, other_core(near, shards)]
        far = along_z(far, shards)
        rows_far += [far, other_core(far, shards)]
    last = along_z(jnp.where(core == 0, near, far), shards)
    return rows_near + rows_far + [last, other_core(last, shards)], early


def in_turn(value, pairs, shards):
    axes = ("section", "fsdp")
    half = value.shape[0] // 2

    def of_core(core):
        return [(a * shards + d, b * shards + d) for a, b in pairs for d in range(core, shards, 2)]

    upper = lax.ppermute(value[:half], axes, of_core(0))
    lower = lax.ppermute(value[half:], axes, of_core(0))
    word = lax.ppermute(
        upper[:8, :128], axes, [(a * shards + d, a * shards + d + 1) for a, _ in pairs for d in range(0, shards, 2)]
    )
    word, value = lax.optimization_barrier((word, value))
    return jnp.concatenate([upper, lower]) + lax.ppermute(value, axes, of_core(1))


def add_kernel(*refs):
    total = refs[0][...].astype(jnp.float32)
    for ref in refs[1:-1]:
        total += ref[...].astype(jnp.float32)
    refs[-1][...] = total.astype(jnp.bfloat16).reshape(refs[-1].shape)


def rounded_sum(*terms):
    block = terms[0][0].shape[1:]

    def spec(at):
        return pl.BlockSpec((1, 1) + block[1:], lambda i: (at, i) + (0,) * (len(block) - 1))

    return pl.pallas_call(
        add_kernel,
        grid=(block[0],),
        in_specs=[spec(at) for _, at in terms],
        out_specs=pl.BlockSpec((1,) + block[1:], lambda i: (i,) + (0,) * (len(block) - 1)),
        out_shape=jax.ShapeDtypeStruct(block, jnp.bfloat16),
        compiler_params=params(),
        name="plus",
    )(*[array for array, _ in terms])


def scatter_sum(keep, first, send, own, shards, core):
    taken_first = other_core(first, shards)
    taken = other_core(send, shards)
    came = along_z(rounded_sum((keep, 0), (taken_first, 0)), shards)
    zero = jnp.zeros_like(came)
    far = rounded_sum((keep, 2), (taken, 1), (jnp.where(core == 1, came, zero)[None], 0))
    near = rounded_sum((keep, 1), (taken, 0), (jnp.where(core == 0, came, zero)[None], 0))
    for k in (1, 2, 3):
        far = along_z(far, shards)
        near = along_z(near, shards)
        far = rounded_sum((far[None], 0), *([(keep, 2 * k + 2), (taken, 2 * k + 1)] if k < 3 else [(own, 1)]))
        near = rounded_sum((near[None], 0), *([(keep, 2 * k + 1), (taken, 2 * k)] if k < 3 else [(own, 0)]))
    far_own = far[0].astype(jnp.float32) + other_core(far[1], shards).astype(jnp.float32)
    far_own = other_y(far_own.astype(jnp.bfloat16), shards).astype(jnp.float32)
    near_own = near[0].astype(jnp.float32) + other_core(near[1], shards).astype(jnp.float32)
    return near_own + far_own


def body(upstream, saved_inputs, queries, keys, segments, weights, gains):
    sections = lax.axis_size("section")
    section_index = lax.axis_index("section")
    shards = lax.axis_size("fsdp")
    batches, length, width = upstream.shape
    rank = weights.shape[3]
    saved = saved_inputs[0]
    seg_row = segments
    seg_col = jnp.transpose(segments, (0, 2, 1))
    bf16, f32 = (jnp.bfloat16, jnp.float32)
    shape = jax.ShapeDtypeStruct
    any_spec = pl.BlockSpec(memory_space=pl.ANY)

    position = lax.axis_index("fsdp").astype(jnp.int32)
    z, y_hi, core = position // 4, position // 2 % 2, position % 2
    chips = shards // 4
    own_rows = weights[0]
    pair = lambda *tail: pl.BlockSpec((1, 1) + tail, lambda l, m: (l, m) + (0,) * len(tail))
    rstd, probs = pl.pallas_call(
        pre_kernel,
        grid=(2, batches),
        in_specs=[
            pair(length, width),
            pair(length, rank),
            pair(length, rank),
            pl.BlockSpec((1, 1, length), lambda l, m: (m, 0, 0)),
            pl.BlockSpec((1, length, 1), lambda l, m: (m, 0, 0)),
        ],
        out_specs=[pair(length, 128), pair(HEADS, length, length)],
        out_shape=[
            shape((2, batches, length, 128), f32),
            shape((2, batches, HEADS, length, length), bf16),
        ],
        compiler_params=params(),
        name="rows_alone",
    )(saved, queries[0], keys[0], seg_row, seg_col)

    gathered, (rstd, probs) = gather_blocks(own_rows, shards, core, (rstd, probs))

    turn = 1 - 2 * core
    starts = []

    def row_of(chip, high, low):
        return chip % chips * 4 * length + high * 2 * length + low * length

    for high in (y_hi, 1 - y_hi):
        starts += [row_of(z, high, core), row_of(z, high, 1 - core)]
        for k in (1, 2, 3):
            starts += [row_of(z - turn * k + chips, high, core), row_of(z - turn * k + chips, high, 1 - core)]
            starts += [row_of(z + turn * k + chips, high, 1 - core), row_of(z + turn * k + chips, high, core)]
    far = y_hi ^ core
    starts += [row_of(z + 4, far, core), row_of(z + 4, far, 1 - core)]
    starts += [row_of(z + 4, 1 - far, 1 - core), row_of(z + 4, 1 - far, core)]
    smem = pl.BlockSpec(memory_space=pltpu.SMEM)
    vmem = pl.BlockSpec(memory_space=pltpu.VMEM)
    hbm = pl.BlockSpec(memory_space=pltpu.HBM)
    grads_shape = shape((2, batches, length, width), bf16)
    dvs_shape = shape((2, batches, length, rank), bf16)
    boundary_shape = shape((batches, length, width), bf16)
    out_shape = shape((length, width), bf16)
    full_weight, vals, mixed, grads, dvs, boundary, incoming = pl.pallas_call(
        value_kernel,
        in_specs=[smem] + [hbm] * (BLOCKS + 1) + [vmem] * 3,
        out_specs=[hbm, vmem, vmem] + [hbm] * 4,
        out_shape=[
            shape((2, width, rank), bf16),
            shape((2, batches, length, rank), f32),
            shape((2, batches, length, rank), bf16),
            grads_shape,
            dvs_shape,
            boundary_shape,
            out_shape,
        ],
        scratch_shapes=[
            pltpu.VMEM((2, width, rank), bf16),
            pltpu.VMEM((2, batches, length, width), bf16),
            pltpu.SemaphoreType.DMA((2, 2 * BLOCKS)),
            pltpu.SemaphoreType.DMA((2,)),
            pltpu.SemaphoreType.DMA((2,)),
        ],
        compiler_params=params(VMEM_VALUES),
        name="values",
    )(jnp.stack(starts), *gathered, saved, rstd, gains[0], probs)

    tick = pl.pallas_call(
        tick_kernel,
        in_specs=[smem] + [hbm] * 11,
        out_specs=[hbm] * 4,
        out_shape=[out_shape, grads_shape, dvs_shape, boundary_shape],
        input_output_aliases={9: 1, 10: 2, 11: 3},
        scratch_shapes=[
            pltpu.VMEM((3, length, width), bf16),
            pltpu.VMEM((2, length, width), bf16),
            pltpu.VMEM((2, width, rank), bf16),
            pltpu.VMEM((2, width), f32),
            pltpu.VMEM((2, HEADS, length, length), bf16),
            pltpu.VMEM((2, length, rank), f32),
            pltpu.VMEM((2, length, 128), f32),
            pltpu.VMEM((2, length, rank), bf16),
            pltpu.SemaphoreType.DMA((40,)),
        ],
        compiler_params=params(VMEM_ALL),
        name="section",
    )

    top = (section_index == sections - 1).astype(jnp.int32)
    for step in range(sections + batches - 1):
        micro = step - (sections - 1 - section_index)
        place = jnp.stack([micro.astype(jnp.int32), top])
        out, grads, dvs, boundary = tick(
            place, incoming, upstream, saved, full_weight, gains[0], probs, vals, rstd,
            grads, dvs, boundary,
        )
        if step < sections + batches - 2:
            senders = [sections - 1 - step + m for m in range(batches)]
            pairs = [(s, s - 1) for s in senders if 1 <= s < sections]
            if step == 0:
                incoming = in_turn(out, pairs, shards)
            else:
                incoming = lax.ppermute(out, "section", pairs)

    def tiles_of(low):
        way = 1 - 2 * low
        tiles = [(z + 4) % chips * 2 + (y_hi ^ low)]
        for k in (3, 2, 1):
            for high in (y_hi, 1 - y_hi):
                tiles.append((z + way * k + chips) % chips * 2 + high)
        return tiles

    right = pl.pallas_call(
        transpose_kernel,
        in_specs=[vmem] * 2,
        out_specs=vmem,
        out_shape=shape((2, rank, 2 * batches * length), bf16),
        compiler_params=params(),
        name="factors",
    )(mixed, dvs)
    block = (2, 2, rank, length)

    def partial(tiles, low, split):
        return pl.pallas_call(
            functools.partial(weight_kernel, split, len(tiles)),
            in_specs=[smem] + [vmem] * 5,
            out_specs=[hbm] * 2,
            out_shape=[shape((split,) + block, bf16), shape((len(tiles) - split,) + block, bf16)],
            scratch_shapes=[pltpu.VMEM((2,) + block, bf16), pltpu.SemaphoreType.DMA((2,))],
            compiler_params=params(),
            name="partial",
        )(jnp.stack(tiles + [low] * len(tiles)), grads, saved, rstd, gains[0], right)

    first, send = partial(tiles_of(1 - core), 1 - core, 1)
    keep, own = partial(tiles_of(core) + [z * 2 + y_hi, z * 2 + 1 - y_hi], core, RING)
    summed = scatter_sum(keep, first, send, own, shards, core)
    weight_grad = (jnp.transpose(summed, (0, 2, 1)) / shards)[None]
    return (boundary[None], weight_grad)


def solution(mesh):
    return jax.shard_map(
        body,
        mesh=mesh,
        in_specs=(
            P(None, "fsdp", None),
            P("section", None, None, "fsdp", None),
            P("section", None, None, "fsdp", None),
            P("section", None, None, "fsdp", None),
            P(None, "fsdp", None),
            P("section", None, "fsdp", None),
            P("section", None, None),
        ),
        out_specs=(P("section", None, "fsdp", None), P("section", None, "fsdp", None)),
        check_vma=False,
    )
```

```python
import functools
import math

import jax
import jax.numpy as jnp
from jax import lax
from jax.experimental import pallas as pl
from jax.experimental.pallas import tpu as pltpu
from jax.sharding import PartitionSpec as P

HEADS = 4
HEAD_DIM = 128
EPS = 1e-05
CHUNK = 512
BLOCKS = 16
RING = 7
VMEM_LIMIT = 20 * 1024 * 1024
VMEM_VALUES = 56 * 1024 * 1024
VMEM_ALL = 62 * 1024 * 1024


def pre_kernel(x_ref, q_ref, k_ref, seg_row_ref, seg_col_ref, rstd_ref, probs_ref):
    length, width = x_ref.shape[2:]
    total = jnp.zeros((length, 1), jnp.float32)
    for at in range(0, width, CHUNK):
        part = x_ref[0, 0, :, at : at + CHUNK].astype(jnp.float32)
        total += jnp.sum(part * part, -1, keepdims=True)
    rstd = lax.rsqrt(total / width + EPS)
    rstd_ref[0, 0] = jnp.broadcast_to(rstd, (length, 128))
    rows = lax.broadcasted_iota(jnp.int32, (length, length), 0)
    columns = lax.broadcasted_iota(jnp.int32, (length, length), 1)
    allowed = (rows >= columns) & (seg_col_ref[0] == seg_row_ref[0])
    for head in range(HEADS):
        own = slice(head * HEAD_DIM, (head + 1) * HEAD_DIM)
        scores = lax.dot_general(
            q_ref[0, 0, :, own],
            k_ref[0, 0, :, own],
            (((1,), (1,)), ((), ())),
            preferred_element_type=jnp.float32,
        ) * (1.0 / math.sqrt(HEAD_DIM))
        scores = jnp.where(allowed, scores, -1e30)
        peak = jnp.max(scores, -1, keepdims=True)
        expo = jnp.where(allowed, jnp.exp(scores - peak), 0.0)
        probs = expo / jnp.sum(expo, -1, keepdims=True)
        probs_ref[0, 0, head] = probs.astype(jnp.bfloat16)


def value_kernel(place_ref, *refs):
    blocks, refs = refs[:BLOCKS], refs[BLOCKS:]
    saved, rstd, gains, probs, weight, vals, mixed, _, _, _, _, w_buf, x_buf, sems, x_sem, out_sem = refs
    batches, length, width = saved.shape[1:]
    rank = w_buf.shape[2]
    x_copies = [
        pltpu.make_async_copy(saved.at[layer], x_buf.at[layer], x_sem.at[layer]) for layer in (0, 1)
    ]
    loads = [[], []]
    rows = blocks[0].shape[2]
    for layer in (1, 0):
        for at, block in enumerate(blocks):
            for slot in (0, 1):
                start = pl.multiple_of(place_ref[2 * at + slot], rows)
                made = pltpu.make_async_copy(
                    block.at[slot, layer],
                    w_buf.at[layer, pl.ds(start, rows)],
                    sems.at[layer, 2 * at + slot],
                )
                made.start()
                loads[layer].append(made)
        x_copies[layer].start()
    stores = []
    for layer in (1, 0):
        for made in loads[layer]:
            made.wait()
        store = pltpu.make_async_copy(w_buf.at[layer], weight.at[layer], out_sem.at[layer])
        store.start()
        stores.append(store)
        x_copies[layer].wait()
        acc = jnp.zeros((batches * length, rank), jnp.float32)
        for at in range(0, width, CHUNK):
            cut = slice(at, at + CHUNK)
            gain = gains[layer : layer + 1, cut]
            normed = [
                (x_buf[layer, m, :, cut].astype(jnp.float32) * rstd[layer, m, :, 0:1] * gain)
                .astype(jnp.bfloat16)
                for m in range(batches)
            ]
            acc += jnp.dot(
                jnp.concatenate(normed, 0),
                w_buf[layer, cut, :],
                preferred_element_type=jnp.float32,
            )
        for m in range(batches):
            part = acc[m * length : (m + 1) * length]
            vals[layer, m] = part
            values = part.astype(jnp.bfloat16)
            for head in range(HEADS):
                own = slice(head * HEAD_DIM, (head + 1) * HEAD_DIM)
                mixed[layer, m, :, own] = jnp.dot(
                    probs[layer, m, head], values[:, own], preferred_element_type=jnp.float32
                ).astype(jnp.bfloat16)
    for store in stores:
        store.wait()


def tick_kernel(
    place_ref, incoming, upstream, saved, weight, gains, probs, vals, rstd,
    grads_in, dvs_in, boundary_in,
    out, grads, dvs, boundary,
    g_buf, x_buf, w_buf, gain_buf, p_buf, v_buf, r_buf, dv_buf, sems,
):
    del grads_in, dvs_in, boundary_in
    micro, top = place_ref[0], place_ref[1]
    batches = upstream.shape[0]
    width = incoming.shape[1]
    rank = weight.shape[2]
    count = width // CHUNK

    @pl.when((micro >= 0) & (micro < batches))
    def _():
        used = [0]

        def copy(source, target):
            made = pltpu.make_async_copy(source, target, sems.at[used[0]])
            used[0] += 1
            return made

        from_top = copy(upstream.at[micro], g_buf.at[0])
        from_above = pltpu.make_async_copy(incoming, g_buf.at[0], sems.at[used[0] - 1])

        @pl.when(top == 1)
        def _():
            from_top.start()

        @pl.when(top == 0)
        def _():
            from_above.start()

        load_w, load_x, load_p, load_v, load_r = ({}, {}, {}, {}, {})
        load_gain = copy(gains, gain_buf)
        for layer in (1, 0):
            for c in range(count):
                rows = pl.ds(c * CHUNK, CHUNK)
                load_w[layer, c] = copy(weight.at[layer, rows], w_buf.at[layer, rows])
            load_p[layer] = copy(probs.at[layer, micro], p_buf.at[layer])
            load_v[layer] = copy(vals.at[layer, micro], v_buf.at[layer])
            load_r[layer] = copy(rstd.at[layer, micro], r_buf.at[layer])
            load_x[layer] = copy(saved.at[layer, micro], x_buf.at[layer])
        for c in range(count):
            load_w[1, c].start()
        for made in (load_p[1], load_v[1], load_r[1], load_gain, load_x[1]):
            made.start()
        for c in range(count):
            load_w[0, c].start()
        for made in (load_p[0], load_v[0], load_r[0], load_x[0]):
            made.start()

        from_top.wait()
        acc = None
        for c in range(count):
            load_w[1, c].wait()
            rows = slice(c * CHUNK, (c + 1) * CHUNK)
            term = jnp.dot(
                g_buf[0, :, rows], w_buf[1, rows, :], preferred_element_type=jnp.float32
            )
            acc = term if acc is None else acc + term
        stores = [copy(g_buf.at[0], grads.at[1, micro])]
        stores[0].start()
        load_gain.wait()
        for step, layer in enumerate((1, 0)):
            dmix = acc.astype(jnp.bfloat16)
            load_p[layer].wait()
            for head in range(HEADS):
                own = slice(head * HEAD_DIM, (head + 1) * HEAD_DIM)
                dv_buf[layer, :, own] = lax.dot_general(
                    p_buf[layer, head],
                    dmix[:, own],
                    (((0,), (0,)), ((), ())),
                    preferred_element_type=jnp.float32,
                ).astype(jnp.bfloat16)
            stores.append(copy(dv_buf.at[layer], dvs.at[layer, micro]))
            stores[-1].start()
            dv = dv_buf[layer]
            load_v[layer].wait()
            load_r[layer].wait()
            scale = r_buf[layer, :, 0:1]
            mean = jnp.sum(dv.astype(jnp.float32) * v_buf[layer], -1, keepdims=True) / width
            pull = scale * scale * mean
            load_x[layer].wait()
            acc = None
            for c in range(count):
                rows = slice(c * CHUNK, (c + 1) * CHUNK)
                dnormed = lax.dot_general(
                    dv, w_buf[layer, rows, :], (((1,), (1,)), ((), ())),
                    preferred_element_type=jnp.float32,
                )
                lower = (
                    g_buf[step, :, rows].astype(jnp.float32)
                    + scale * (dnormed * gain_buf[layer : layer + 1, rows])
                    - x_buf[layer, :, rows].astype(jnp.float32) * pull
                ).astype(jnp.bfloat16)
                g_buf[step + 1, :, rows] = lower
                if layer == 1:
                    load_w[0, c].wait()
                    term = jnp.dot(
                        lower, w_buf[0, rows, :], preferred_element_type=jnp.float32
                    )
                    acc = term if acc is None else acc + term
            if layer == 1:
                stores.append(copy(g_buf.at[1], grads.at[0, micro]))
                stores[-1].start()
        stores.append(copy(g_buf.at[2], out))
        stores[-1].start()
        stores.append(copy(g_buf.at[2], boundary.at[micro]))
        stores[-1].start()
        for store in stores:
            store.wait()


def transpose_kernel(mixed_ref, dv_ref, right_ref):
    batches, length = mixed_ref.shape[1:3]
    rows = batches * length
    for layer in (0, 1):
        for m in range(batches):
            at = m * length
            right_ref[layer, :, at : at + length] = mixed_ref[layer, m].T
            right_ref[layer, :, rows + at : rows + at + length] = dv_ref[layer, m].T


def weight_kernel(counts, place_ref, g_ref, x_ref, rstd_ref, gain_ref, right_ref, *refs):
    outs, (buf, sems) = refs[: len(counts)], refs[len(counts) :]
    tiles = sum(counts)
    batches, length = g_ref.shape[1:3]
    wide = 2 * length

    def store(tile, slot, target, at):
        return pltpu.make_async_copy(buf.at[slot], target.at[at], sems.at[slot])

    def step(tile, carry):
        slot = lax.rem(tile, 2)
        start = pl.multiple_of(place_ref[tile] * wide, wide)
        cut = pl.ds(start, wide)

        @pl.when(tile >= 2)
        def _():
            store(tile, slot, outs[0], 0).wait()

        for layer in (0, 1):
            left = [g_ref[layer, m, :, cut] for m in range(batches)]
            left += [
                (
                    x_ref[layer, m, :, cut].astype(jnp.float32)
                    * rstd_ref[layer, m, :, 0:1]
                    * gain_ref[layer : layer + 1, cut]
                ).astype(jnp.bfloat16)
                for m in range(batches)
            ]
            result = jnp.dot(
                right_ref[layer], jnp.concatenate(left, 0), preferred_element_type=jnp.float32
            ).astype(jnp.bfloat16)
            turned = place_ref[tiles + tile]
            buf[slot, turned, layer] = result[:, :length]
            buf[slot, 1 - turned, layer] = result[:, length:]

        low = 0
        for count, out in zip(counts, outs):

            @pl.when((tile >= low) & (tile < low + count))
            def _(low=low, count=count, out=out):
                store(tile, slot, out, jnp.clip(tile - low, 0, count - 1)).start()

            low += count

        return carry

    lax.fori_loop(0, tiles, step, 0)
    for tile in (tiles - 2, tiles - 1):
        store(tile, tile % 2, outs[0], 0).wait()


def params(limit=VMEM_LIMIT):
    return pltpu.CompilerParams(vmem_limit_bytes=limit)


def other_core(value, shards):
    return lax.ppermute(value, "fsdp", [(d, d ^ 1) for d in range(shards)])


def other_y(value, shards):
    return lax.ppermute(value, "fsdp", [(d, d ^ 2) for d in range(shards)])


def along_z(value, shards):
    return lax.ppermute(
        value, "fsdp", [(d, (d + (4 if d % 2 == 0 else shards - 4)) % shards) for d in range(shards)]
    )


def gather_blocks(own_rows, shards, core, early):
    near = jnp.stack([own_rows, other_core(own_rows, shards)])
    rows_near = [near]
    far_rows = other_y(own_rows, shards)
    near = along_z(near, shards)
    near, far_rows = lax.optimization_barrier((near, far_rows))
    rows_near += [near, other_core(near, shards)]
    far = jnp.stack([far_rows, other_core(far_rows, shards)])
    rows_far = [far]
    for k in (1, 2, 3):
        if k == 2:
            far, early = lax.optimization_barrier((far, early))
        if k > 1:
            near = along_z(near, shards)
            rows_near += [near, other_core(near, shards)]
        far = along_z(far, shards)
        rows_far += [far, other_core(far, shards)]
    last = along_z(jnp.where(core == 0, near, far), shards)
    return rows_near + rows_far + [last, other_core(last, shards)], early


def wait_kernel(value_ref, word_ref, out_ref):
    del value_ref, word_ref, out_ref


def in_turn(value, pairs, shards):
    axes = ("section", "fsdp")

    def of_core(core):
        return [(a * shards + d, b * shards + d) for a, b in pairs for d in range(core, shards, 2)]

    lead = lax.ppermute(value, axes, of_core(0))
    word = lax.ppermute(
        lead[:8, :128], axes, [(a * shards + d, a * shards + d + 1) for a, _ in pairs for d in range(0, shards, 2)]
    )
    hbm = pl.BlockSpec(memory_space=pltpu.HBM)
    value = pl.pallas_call(
        wait_kernel,
        in_specs=[hbm, hbm],
        out_specs=hbm,
        out_shape=jax.ShapeDtypeStruct(value.shape, value.dtype),
        input_output_aliases={0: 0},
        compiler_params=params(),
        name="turn",
    )(value, word)
    return lead + lax.ppermute(value, axes, of_core(1))


def add_kernel(*refs):
    total = refs[0][...].astype(jnp.float32)
    for ref in refs[1:-1]:
        total += ref[...].astype(jnp.float32)
    refs[-1][...] = total.astype(jnp.bfloat16).reshape(refs[-1].shape)


def rounded_sum(*terms):
    block = terms[0][0].shape[1:]

    def spec(at):
        return pl.BlockSpec((1, 1) + block[1:], lambda i: (at, i) + (0,) * (len(block) - 1))

    return pl.pallas_call(
        add_kernel,
        grid=(block[0],),
        in_specs=[spec(at) for _, at in terms],
        out_specs=pl.BlockSpec((1,) + block[1:], lambda i: (i,) + (0,) * (len(block) - 1)),
        out_shape=jax.ShapeDtypeStruct(block, jnp.bfloat16),
        compiler_params=params(),
        name="plus",
    )(*[array for array, _ in terms])


def scatter_sum(keep, first, send, own, shards, core):
    taken_first = other_core(first, shards)
    taken = other_core(send, shards)
    came = along_z(rounded_sum((keep, 0), (taken_first, 0)), shards)
    zero = jnp.zeros_like(came)
    far = rounded_sum((keep, 2), (taken, 1), (jnp.where(core == 1, came, zero)[None], 0))
    near = rounded_sum((keep, 1), (taken, 0), (jnp.where(core == 0, came, zero)[None], 0))
    for k in (1, 2, 3):
        far = along_z(far, shards)
        near = along_z(near, shards)
        far = rounded_sum((far[None], 0), *([(keep, 2 * k + 2), (taken, 2 * k + 1)] if k < 3 else [(own, 1)]))
        near = rounded_sum((near[None], 0), *([(keep, 2 * k + 1), (taken, 2 * k)] if k < 3 else [(own, 0)]))
    far_own = far[0].astype(jnp.float32) + other_core(far[1], shards).astype(jnp.float32)
    far_own = other_y(far_own.astype(jnp.bfloat16), shards).astype(jnp.float32)
    near_own = near[0].astype(jnp.float32) + other_core(near[1], shards).astype(jnp.float32)
    return near_own + far_own


def body(upstream, saved_inputs, queries, keys, segments, weights, gains):
    sections = lax.axis_size("section")
    section_index = lax.axis_index("section")
    shards = lax.axis_size("fsdp")
    batches, length, width = upstream.shape
    rank = weights.shape[3]
    saved = saved_inputs[0]
    seg_row = segments
    seg_col = jnp.transpose(segments, (0, 2, 1))
    bf16, f32 = (jnp.bfloat16, jnp.float32)
    shape = jax.ShapeDtypeStruct
    any_spec = pl.BlockSpec(memory_space=pl.ANY)

    position = lax.axis_index("fsdp").astype(jnp.int32)
    z, y_hi, core = position // 4, position // 2 % 2, position % 2
    chips = shards // 4
    own_rows = weights[0]
    pair = lambda *tail: pl.BlockSpec((1, 1) + tail, lambda l, m: (l, m) + (0,) * len(tail))
    rstd, probs = pl.pallas_call(
        pre_kernel,
        grid=(2, batches),
        in_specs=[
            pair(length, width),
            pair(length, rank),
            pair(length, rank),
            pl.BlockSpec((1, 1, length), lambda l, m: (m, 0, 0)),
            pl.BlockSpec((1, length, 1), lambda l, m: (m, 0, 0)),
        ],
        out_specs=[pair(length, 128), pair(HEADS, length, length)],
        out_shape=[
            shape((2, batches, length, 128), f32),
            shape((2, batches, HEADS, length, length), bf16),
        ],
        compiler_params=params(),
        name="rows_alone",
    )(saved, queries[0], keys[0], seg_row, seg_col)

    gathered, (rstd, probs) = gather_blocks(own_rows, shards, core, (rstd, probs))

    turn = 1 - 2 * core
    starts = []

    def row_of(chip, high, low):
        return chip % chips * 4 * length + high * 2 * length + low * length

    for high in (y_hi, 1 - y_hi):
        starts += [row_of(z, high, core), row_of(z, high, 1 - core)]
        for k in (1, 2, 3):
            starts += [row_of(z - turn * k + chips, high, core), row_of(z - turn * k + chips, high, 1 - core)]
            starts += [row_of(z + turn * k + chips, high, 1 - core), row_of(z + turn * k + chips, high, core)]
    far = y_hi ^ core
    starts += [row_of(z + 4, far, core), row_of(z + 4, far, 1 - core)]
    starts += [row_of(z + 4, 1 - far, 1 - core), row_of(z + 4, 1 - far, core)]
    smem = pl.BlockSpec(memory_space=pltpu.SMEM)
    vmem = pl.BlockSpec(memory_space=pltpu.VMEM)
    hbm = pl.BlockSpec(memory_space=pltpu.HBM)
    grads_shape = shape((2, batches, length, width), bf16)
    dvs_shape = shape((2, batches, length, rank), bf16)
    boundary_shape = shape((batches, length, width), bf16)
    out_shape = shape((length, width), bf16)
    full_weight, vals, mixed, grads, dvs, boundary, incoming = pl.pallas_call(
        value_kernel,
        in_specs=[smem] + [hbm] * (BLOCKS + 1) + [vmem] * 3,
        out_specs=[hbm, vmem, vmem] + [hbm] * 4,
        out_shape=[
            shape((2, width, rank), bf16),
            shape((2, batches, length, rank), f32),
            shape((2, batches, length, rank), bf16),
            grads_shape,
            dvs_shape,
            boundary_shape,
            out_shape,
        ],
        scratch_shapes=[
            pltpu.VMEM((2, width, rank), bf16),
            pltpu.VMEM((2, batches, length, width), bf16),
            pltpu.SemaphoreType.DMA((2, 2 * BLOCKS)),
            pltpu.SemaphoreType.DMA((2,)),
            pltpu.SemaphoreType.DMA((2,)),
        ],
        compiler_params=params(VMEM_VALUES),
        name="values",
    )(jnp.stack(starts), *gathered, saved, rstd, gains[0], probs)

    tick = pl.pallas_call(
        tick_kernel,
        in_specs=[smem] + [hbm] * 11,
        out_specs=[hbm] * 4,
        out_shape=[out_shape, grads_shape, dvs_shape, boundary_shape],
        input_output_aliases={9: 1, 10: 2, 11: 3},
        scratch_shapes=[
            pltpu.VMEM((3, length, width), bf16),
            pltpu.VMEM((2, length, width), bf16),
            pltpu.VMEM((2, width, rank), bf16),
            pltpu.VMEM((2, width), f32),
            pltpu.VMEM((2, HEADS, length, length), bf16),
            pltpu.VMEM((2, length, rank), f32),
            pltpu.VMEM((2, length, 128), f32),
            pltpu.VMEM((2, length, rank), bf16),
            pltpu.SemaphoreType.DMA((40,)),
        ],
        compiler_params=params(VMEM_ALL),
        name="section",
    )

    top = (section_index == sections - 1).astype(jnp.int32)
    for step in range(sections + batches - 1):
        micro = step - (sections - 1 - section_index)
        place = jnp.stack([micro.astype(jnp.int32), top])
        out, grads, dvs, boundary = tick(
            place, incoming, upstream, saved, full_weight, gains[0], probs, vals, rstd,
            grads, dvs, boundary,
        )
        if step < sections + batches - 2:
            senders = [sections - 1 - step + m for m in range(batches)]
            pairs = [(s, s - 1) for s in senders if 1 <= s < sections]
            if step == 0:
                incoming = in_turn(out, pairs, shards)
            else:
                incoming = lax.ppermute(out, "section", pairs)

    def tiles_of(low):
        way = 1 - 2 * low
        tiles = [(z + 4) % chips * 2 + (y_hi ^ low)]
        for k in (3, 2, 1):
            for high in (y_hi, 1 - y_hi):
                tiles.append((z + way * k + chips) % chips * 2 + high)
        return tiles

    right = pl.pallas_call(
        transpose_kernel,
        in_specs=[vmem] * 2,
        out_specs=vmem,
        out_shape=shape((2, rank, 2 * batches * length), bf16),
        compiler_params=params(),
        name="factors",
    )(mixed, dvs)
    block = (2, 2, rank, length)

    counts = (1, RING - 1, RING, 2)
    tiles = tiles_of(1 - core) + tiles_of(core) + [z * 2 + y_hi, z * 2 + 1 - y_hi]
    flips = [1 - core] * RING + [core] * (RING + 2)
    first, send, keep, own = pl.pallas_call(
        functools.partial(weight_kernel, counts),
        in_specs=[smem] + [vmem] * 5,
        out_specs=[hbm] * 4,
        out_shape=[shape((count,) + block, bf16) for count in counts],
        scratch_shapes=[pltpu.VMEM((2,) + block, bf16), pltpu.SemaphoreType.DMA((2,))],
        compiler_params=params(),
        name="partial",
    )(jnp.stack(tiles + flips), grads, saved, rstd, gains[0], right)
    summed = scatter_sum(keep, first, send, own, shards, core)
    weight_grad = (jnp.transpose(summed, (0, 2, 1)) / shards)[None]
    return (boundary[None], weight_grad)


def solution(mesh):
    return jax.shard_map(
        body,
        mesh=mesh,
        in_specs=(
            P(None, "fsdp", None),
            P("section", None, None, "fsdp", None),
            P("section", None, None, "fsdp", None),
            P("section", None, None, "fsdp", None),
            P(None, "fsdp", None),
            P("section", None, "fsdp", None),
            P("section", None, None),
        ),
        out_specs=(P("section", None, "fsdp", None), P("section", None, "fsdp", None)),
        check_vma=False,
    )
```

```python
import functools
import math

import jax
import jax.numpy as jnp
from jax import lax
from jax.experimental import pallas as pl
from jax.experimental.pallas import tpu as pltpu
from jax.sharding import PartitionSpec as P

HEADS = 4
HEAD_DIM = 128
EPS = 1e-05
CHUNK = 512
BLOCKS = 16
RING = 7
VMEM_LIMIT = 20 * 1024 * 1024
VMEM_VALUES = 56 * 1024 * 1024
VMEM_ALL = 62 * 1024 * 1024
VMEM_TICK = 58 * 1024 * 1024
VMEM_PLUS = 20 * 1024 * 1024


def pre_kernel(x_ref, q_ref, k_ref, seg_row_ref, seg_col_ref, rstd_ref, probs_ref):
    length, width = x_ref.shape[2:]
    total = jnp.zeros((length, 1), jnp.float32)
    for at in range(0, width, CHUNK):
        part = x_ref[0, 0, :, at : at + CHUNK].astype(jnp.float32)
        total += jnp.sum(part * part, -1, keepdims=True)
    rstd = lax.rsqrt(total / width + EPS)
    rstd_ref[0, 0] = jnp.broadcast_to(rstd, (length, 128))
    rows = lax.broadcasted_iota(jnp.int32, (length, length), 0)
    columns = lax.broadcasted_iota(jnp.int32, (length, length), 1)
    allowed = (rows >= columns) & (seg_col_ref[0] == seg_row_ref[0])
    for head in range(HEADS):
        own = slice(head * HEAD_DIM, (head + 1) * HEAD_DIM)
        scores = lax.dot_general(
            q_ref[0, 0, :, own],
            k_ref[0, 0, :, own],
            (((1,), (1,)), ((), ())),
            preferred_element_type=jnp.float32,
        ) * (1.0 / math.sqrt(HEAD_DIM))
        scores = jnp.where(allowed, scores, -1e30)
        peak = jnp.max(scores, -1, keepdims=True)
        expo = jnp.where(allowed, jnp.exp(scores - peak), 0.0)
        probs = expo / jnp.sum(expo, -1, keepdims=True)
        probs_ref[0, 0, head] = probs.astype(jnp.bfloat16)


def value_kernel(place_ref, *refs):
    blocks, refs = refs[:BLOCKS], refs[BLOCKS:]
    saved, rstd, gains, probs, weight, vals, mixed, _, _, _, _, w_buf, x_buf, sems, x_sem, out_sem = refs
    batches, length, width = saved.shape[1:]
    rank = w_buf.shape[2]
    x_copies = [
        pltpu.make_async_copy(saved.at[layer], x_buf.at[layer], x_sem.at[layer]) for layer in (0, 1)
    ]
    loads = [[], []]
    rows = blocks[0].shape[2]
    for layer in (1, 0):
        for at, block in enumerate(blocks):
            for slot in (0, 1):
                start = pl.multiple_of(place_ref[2 * at + slot], rows)
                made = pltpu.make_async_copy(
                    block.at[slot, layer],
                    w_buf.at[layer, pl.ds(start, rows)],
                    sems.at[layer, 2 * at + slot],
                )
                made.start()
                loads[layer].append(made)
        x_copies[layer].start()
    stores = []
    for layer in (1, 0):
        for made in loads[layer]:
            made.wait()
        store = pltpu.make_async_copy(w_buf.at[layer], weight.at[layer], out_sem.at[layer])
        store.start()
        stores.append(store)
        x_copies[layer].wait()
        acc = jnp.zeros((batches * length, rank), jnp.float32)
        for at in range(0, width, CHUNK):
            cut = slice(at, at + CHUNK)
            gain = gains[layer : layer + 1, cut]
            normed = [
                (x_buf[layer, m, :, cut].astype(jnp.float32) * rstd[layer, m, :, 0:1] * gain)
                .astype(jnp.bfloat16)
                for m in range(batches)
            ]
            acc += jnp.dot(
                jnp.concatenate(normed, 0),
                w_buf[layer, cut, :],
                preferred_element_type=jnp.float32,
            )
        for m in range(batches):
            part = acc[m * length : (m + 1) * length]
            vals[layer, m] = part
            values = part.astype(jnp.bfloat16)
            for head in range(HEADS):
                own = slice(head * HEAD_DIM, (head + 1) * HEAD_DIM)
                mixed[layer, m, :, own] = jnp.dot(
                    probs[layer, m, head], values[:, own], preferred_element_type=jnp.float32
                ).astype(jnp.bfloat16)
    for store in stores:
        store.wait()


def tick_kernel(
    place_ref, incoming, upstream, saved, weight, gains, probs, vals, rstd,
    grads_in, dvs_in, boundary_in,
    out, grads, dvs, boundary,
    g_buf, x_buf, w_buf, gain_buf, p_buf, v_buf, r_buf, dv_buf, sems,
):
    del grads_in, dvs_in, boundary_in
    micro, top = place_ref[0], place_ref[1]
    batches = upstream.shape[0]
    width = incoming.shape[1]
    rank = weight.shape[2]
    count = width // CHUNK

    @pl.when((micro >= 0) & (micro < batches))
    def _():
        used = [0]

        def copy(source, target):
            made = pltpu.make_async_copy(source, target, sems.at[used[0]])
            used[0] += 1
            return made

        from_top = copy(upstream.at[micro], g_buf.at[0])
        from_above = pltpu.make_async_copy(incoming, g_buf.at[0], sems.at[used[0] - 1])

        @pl.when(top == 1)
        def _():
            from_top.start()

        @pl.when(top == 0)
        def _():
            from_above.start()

        load_w, load_x, load_p, load_v, load_r = ({}, {}, {}, {}, {})
        load_gain = copy(gains, gain_buf)
        for layer in (1, 0):
            for c in range(count):
                rows = pl.ds(c * CHUNK, CHUNK)
                load_w[layer, c] = copy(weight.at[layer, rows], w_buf.at[layer, rows])
            load_p[layer] = copy(probs.at[layer, micro], p_buf.at[layer])
            load_v[layer] = copy(vals.at[layer, micro], v_buf.at[layer])
            load_r[layer] = copy(rstd.at[layer, micro], r_buf.at[layer])
            load_x[layer] = copy(saved.at[layer, micro], x_buf.at[layer])
        for c in range(count):
            load_w[1, c].start()
        for made in (load_p[1], load_v[1], load_r[1], load_gain, load_x[1]):
            made.start()
        for c in range(count):
            load_w[0, c].start()
        for made in (load_p[0], load_v[0], load_r[0], load_x[0]):
            made.start()

        from_top.wait()
        acc = None
        for c in range(count):
            load_w[1, c].wait()
            rows = slice(c * CHUNK, (c + 1) * CHUNK)
            term = jnp.dot(
                g_buf[0, :, rows], w_buf[1, rows, :], preferred_element_type=jnp.float32
            )
            acc = term if acc is None else acc + term
        stores = [copy(g_buf.at[0], grads.at[1, micro])]
        stores[0].start()
        load_gain.wait()
        for step, layer in enumerate((1, 0)):
            dmix = acc.astype(jnp.bfloat16)
            load_p[layer].wait()
            for head in range(HEADS):
                own = slice(head * HEAD_DIM, (head + 1) * HEAD_DIM)
                dv_buf[layer, :, own] = lax.dot_general(
                    p_buf[layer, head],
                    dmix[:, own],
                    (((0,), (0,)), ((), ())),
                    preferred_element_type=jnp.float32,
                ).astype(jnp.bfloat16)
            stores.append(copy(dv_buf.at[layer], dvs.at[layer, micro]))
            stores[-1].start()
            dv = dv_buf[layer]
            load_v[layer].wait()
            load_r[layer].wait()
            scale = r_buf[layer, :, 0:1]
            mean = jnp.sum(dv.astype(jnp.float32) * v_buf[layer], -1, keepdims=True) / width
            pull = scale * scale * mean
            load_x[layer].wait()
            acc = None
            for c in range(count):
                rows = slice(c * CHUNK, (c + 1) * CHUNK)
                dnormed = lax.dot_general(
                    dv, w_buf[layer, rows, :], (((1,), (1,)), ((), ())),
                    preferred_element_type=jnp.float32,
                )
                lower = (
                    g_buf[step, :, rows].astype(jnp.float32)
                    + scale * (dnormed * gain_buf[layer : layer + 1, rows])
                    - x_buf[layer, :, rows].astype(jnp.float32) * pull
                ).astype(jnp.bfloat16)
                g_buf[step + 1, :, rows] = lower
                if layer == 1:
                    load_w[0, c].wait()
                    term = jnp.dot(
                        lower, w_buf[0, rows, :], preferred_element_type=jnp.float32
                    )
                    acc = term if acc is None else acc + term
            if layer == 1:
                stores.append(copy(g_buf.at[1], grads.at[0, micro]))
                stores[-1].start()
        stores.append(copy(g_buf.at[2], out))
        stores[-1].start()
        stores.append(copy(g_buf.at[2], boundary.at[micro]))
        stores[-1].start()
        for store in stores:
            store.wait()


def transpose_kernel(mixed_ref, dv_ref, right_ref):
    batches, length = mixed_ref.shape[1:3]
    rows = batches * length
    for layer in (0, 1):
        for m in range(batches):
            at = m * length
            right_ref[layer, :, at : at + length] = mixed_ref[layer, m].T
            right_ref[layer, :, rows + at : rows + at + length] = dv_ref[layer, m].T


def weight_kernel(counts, place_ref, g_ref, x_ref, rstd_ref, gain_ref, right_ref, *refs):
    outs, (buf, sems) = refs[: len(counts)], refs[len(counts) :]
    tiles = sum(counts)
    batches, length = g_ref.shape[1:3]
    wide = 2 * length

    def store(tile, slot, target, at):
        return pltpu.make_async_copy(buf.at[slot], target.at[at], sems.at[slot])

    def step(tile, carry):
        slot = lax.rem(tile, 2)
        start = pl.multiple_of(place_ref[tile] * wide, wide)
        cut = pl.ds(start, wide)

        @pl.when(tile >= 2)
        def _():
            store(tile, slot, outs[0], 0).wait()

        for layer in (0, 1):
            left = [g_ref[layer, m, :, cut] for m in range(batches)]
            left += [
                (
                    x_ref[layer, m, :, cut].astype(jnp.float32)
                    * rstd_ref[layer, m, :, 0:1]
                    * gain_ref[layer : layer + 1, cut]
                ).astype(jnp.bfloat16)
                for m in range(batches)
            ]
            result = jnp.dot(
                right_ref[layer], jnp.concatenate(left, 0), preferred_element_type=jnp.float32
            ).astype(jnp.bfloat16)
            turned = place_ref[tiles + tile]
            buf[slot, turned, layer] = result[:, :length]
            buf[slot, 1 - turned, layer] = result[:, length:]

        low = 0
        for count, out in zip(counts, outs):

            @pl.when((tile >= low) & (tile < low + count))
            def _(low=low, count=count, out=out):
                store(tile, slot, out, jnp.clip(tile - low, 0, count - 1)).start()

            low += count

        return carry

    lax.fori_loop(0, tiles, step, 0)
    for tile in (tiles - 2, tiles - 1):
        store(tile, tile % 2, outs[0], 0).wait()


def params(limit=VMEM_LIMIT):
    return pltpu.CompilerParams(vmem_limit_bytes=limit)


def other_core(value, shards):
    return lax.ppermute(value, "fsdp", [(d, d ^ 1) for d in range(shards)])


def other_y(value, shards):
    return lax.ppermute(value, "fsdp", [(d, d ^ 2) for d in range(shards)])


def along_z(value, shards):
    return lax.ppermute(
        value, "fsdp", [(d, (d + (4 if d % 2 == 0 else shards - 4)) % shards) for d in range(shards)]
    )


def gather_blocks(own_rows, shards, core, early):
    near = jnp.stack([own_rows, other_core(own_rows, shards)])
    rows_near = [near]
    far_rows = other_y(own_rows, shards)
    near = along_z(near, shards)
    near, far_rows = lax.optimization_barrier((near, far_rows))
    rows_near += [near, other_core(near, shards)]
    far = jnp.stack([far_rows, other_core(far_rows, shards)])
    rows_far = [far]
    for k in (1, 2, 3):
        if k == 2:
            far, early = lax.optimization_barrier((far, early))
        if k > 1:
            near = along_z(near, shards)
            rows_near += [near, other_core(near, shards)]
        far = along_z(far, shards)
        rows_far += [far, other_core(far, shards)]
    last = along_z(jnp.where(core == 0, near, far), shards)
    return rows_near + rows_far + [last, other_core(last, shards)], early


def wait_kernel(value_ref, word_ref, out_ref):
    del value_ref, word_ref, out_ref


def in_turn(value, pairs, shards):
    axes = ("section", "fsdp")

    def of_core(core):
        return [(a * shards + d, b * shards + d) for a, b in pairs for d in range(core, shards, 2)]

    lead = lax.ppermute(value, axes, of_core(0))
    word = lax.ppermute(
        lead[:8, :128], axes, [(a * shards + d, a * shards + d + 1) for a, _ in pairs for d in range(0, shards, 2)]
    )
    hbm = pl.BlockSpec(memory_space=pltpu.HBM)
    value = pl.pallas_call(
        wait_kernel,
        in_specs=[hbm, hbm],
        out_specs=hbm,
        out_shape=jax.ShapeDtypeStruct(value.shape, value.dtype),
        input_output_aliases={0: 0},
        compiler_params=params(),
        name="turn",
    )(value, word)
    return lead + lax.ppermute(value, axes, of_core(1))


def add_kernel(*refs):
    total = refs[0][...].astype(jnp.float32)
    for ref in refs[1:-1]:
        total += ref[...].astype(jnp.float32)
    refs[-1][...] = total.astype(jnp.bfloat16).reshape(refs[-1].shape)


def rounded_sum(*terms):
    block = terms[0][0].shape[1:]

    def spec(at):
        return pl.BlockSpec((1, 1) + block[1:], lambda i: (at, i) + (0,) * (len(block) - 1))

    return pl.pallas_call(
        add_kernel,
        grid=(block[0],),
        in_specs=[spec(at) for _, at in terms],
        out_specs=pl.BlockSpec((1,) + block[1:], lambda i: (i,) + (0,) * (len(block) - 1)),
        out_shape=jax.ShapeDtypeStruct(block, jnp.bfloat16),
        compiler_params=params(VMEM_PLUS),
        name="plus",
    )(*[array for array, _ in terms])


def scatter_sum(keep, first, send, own, shards, core):
    taken_first = other_core(first, shards)
    taken = other_core(send, shards)
    came = along_z(rounded_sum((keep, 0), (taken_first, 0)), shards)
    zero = jnp.zeros_like(came)
    near = rounded_sum((keep, 1), (taken, 0), (jnp.where(core == 0, came, zero)[None], 0))
    far = rounded_sum((keep, 2), (taken, 1), (jnp.where(core == 1, came, zero)[None], 0))
    for k in (1, 2, 3):
        near = along_z(near, shards)
        far = along_z(far, shards)
        near = rounded_sum((near[None], 0), *([(keep, 2 * k + 1), (taken, 2 * k)] if k < 3 else [(own, 0)]))
        far = rounded_sum((far[None], 0), *([(keep, 2 * k + 2), (taken, 2 * k + 1)] if k < 3 else [(own, 1)]))
    far_own = far[0].astype(jnp.float32) + other_core(far[1], shards).astype(jnp.float32)
    far_own = other_y(far_own.astype(jnp.bfloat16), shards).astype(jnp.float32)
    near_own = near[0].astype(jnp.float32) + other_core(near[1], shards).astype(jnp.float32)
    return near_own + far_own


def body(upstream, saved_inputs, queries, keys, segments, weights, gains):
    sections = lax.axis_size("section")
    section_index = lax.axis_index("section")
    shards = lax.axis_size("fsdp")
    batches, length, width = upstream.shape
    rank = weights.shape[3]
    saved = saved_inputs[0]
    seg_row = segments
    seg_col = jnp.transpose(segments, (0, 2, 1))
    bf16, f32 = (jnp.bfloat16, jnp.float32)
    shape = jax.ShapeDtypeStruct
    any_spec = pl.BlockSpec(memory_space=pl.ANY)

    position = lax.axis_index("fsdp").astype(jnp.int32)
    z, y_hi, core = position // 4, position // 2 % 2, position % 2
    chips = shards // 4
    own_rows = weights[0]
    pair = lambda *tail: pl.BlockSpec((1, 1) + tail, lambda l, m: (l, m) + (0,) * len(tail))
    rstd, probs = pl.pallas_call(
        pre_kernel,
        grid=(2, batches),
        in_specs=[
            pair(length, width),
            pair(length, rank),
            pair(length, rank),
            pl.BlockSpec((1, 1, length), lambda l, m: (m, 0, 0)),
            pl.BlockSpec((1, length, 1), lambda l, m: (m, 0, 0)),
        ],
        out_specs=[pair(length, 128), pair(HEADS, length, length)],
        out_shape=[
            shape((2, batches, length, 128), f32),
            shape((2, batches, HEADS, length, length), bf16),
        ],
        compiler_params=params(),
        name="rows_alone",
    )(saved, queries[0], keys[0], seg_row, seg_col)

    gathered, (rstd, probs) = gather_blocks(own_rows, shards, core, (rstd, probs))

    turn = 1 - 2 * core
    starts = []

    def row_of(chip, high, low):
        return chip % chips * 4 * length + high * 2 * length + low * length

    for high in (y_hi, 1 - y_hi):
        starts += [row_of(z, high, core), row_of(z, high, 1 - core)]
        for k in (1, 2, 3):
            starts += [row_of(z - turn * k + chips, high, core), row_of(z - turn * k + chips, high, 1 - core)]
            starts += [row_of(z + turn * k + chips, high, 1 - core), row_of(z + turn * k + chips, high, core)]
    far = y_hi ^ core
    starts += [row_of(z + 4, far, core), row_of(z + 4, far, 1 - core)]
    starts += [row_of(z + 4, 1 - far, 1 - core), row_of(z + 4, 1 - far, core)]
    smem = pl.BlockSpec(memory_space=pltpu.SMEM)
    vmem = pl.BlockSpec(memory_space=pltpu.VMEM)
    hbm = pl.BlockSpec(memory_space=pltpu.HBM)
    grads_shape = shape((2, batches, length, width), bf16)
    dvs_shape = shape((2, batches, length, rank), bf16)
    boundary_shape = shape((batches, length, width), bf16)
    out_shape = shape((length, width), bf16)
    full_weight, vals, mixed, grads, dvs, boundary, incoming = pl.pallas_call(
        value_kernel,
        in_specs=[smem] + [hbm] * (BLOCKS + 1) + [vmem] * 3,
        out_specs=[hbm, vmem, vmem] + [hbm] * 4,
        out_shape=[
            shape((2, width, rank), bf16),
            shape((2, batches, length, rank), f32),
            shape((2, batches, length, rank), bf16),
            grads_shape,
            dvs_shape,
            boundary_shape,
            out_shape,
        ],
        scratch_shapes=[
            pltpu.VMEM((2, width, rank), bf16),
            pltpu.VMEM((2, batches, length, width), bf16),
            pltpu.SemaphoreType.DMA((2, 2 * BLOCKS)),
            pltpu.SemaphoreType.DMA((2,)),
            pltpu.SemaphoreType.DMA((2,)),
        ],
        compiler_params=params(VMEM_VALUES),
        name="values",
    )(jnp.stack(starts), *gathered, saved, rstd, gains[0], probs)

    tick = pl.pallas_call(
        tick_kernel,
        in_specs=[smem, any_spec] + [hbm] * 10,
        out_specs=[hbm] * 4,
        out_shape=[out_shape, grads_shape, dvs_shape, boundary_shape],
        input_output_aliases={9: 1, 10: 2, 11: 3},
        scratch_shapes=[
            pltpu.VMEM((3, length, width), bf16),
            pltpu.VMEM((2, length, width), bf16),
            pltpu.VMEM((2, width, rank), bf16),
            pltpu.VMEM((2, width), f32),
            pltpu.VMEM((2, HEADS, length, length), bf16),
            pltpu.VMEM((2, length, rank), f32),
            pltpu.VMEM((2, length, 128), f32),
            pltpu.VMEM((2, length, rank), bf16),
            pltpu.SemaphoreType.DMA((40,)),
        ],
        compiler_params=params(VMEM_TICK),
        name="section",
    )

    top = (section_index == sections - 1).astype(jnp.int32)
    for step in range(sections + batches - 1):
        micro = step - (sections - 1 - section_index)
        place = jnp.stack([micro.astype(jnp.int32), top])
        out, grads, dvs, boundary = tick(
            place, incoming, upstream, saved, full_weight, gains[0], probs, vals, rstd,
            grads, dvs, boundary,
        )
        if step < sections + batches - 2:
            senders = [sections - 1 - step + m for m in range(batches)]
            pairs = [(s, s - 1) for s in senders if 1 <= s < sections]
            if step == 0:
                incoming = in_turn(out, pairs, shards)
            else:
                incoming = lax.ppermute(out, "section", pairs)

    def tiles_of(low):
        way = 1 - 2 * low
        tiles = [(z + 4) % chips * 2 + (y_hi ^ low)]
        for k in (3, 2, 1):
            for high in (y_hi, 1 - y_hi):
                tiles.append((z + way * k + chips) % chips * 2 + high)
        return tiles

    right = pl.pallas_call(
        transpose_kernel,
        in_specs=[vmem] * 2,
        out_specs=vmem,
        out_shape=shape((2, rank, 2 * batches * length), bf16),
        compiler_params=params(),
        name="factors",
    )(mixed, dvs)
    block = (2, 2, rank, length)

    counts = (1, RING - 1, RING, 2)
    tiles = tiles_of(1 - core) + tiles_of(core) + [z * 2 + y_hi, z * 2 + 1 - y_hi]
    flips = [1 - core] * RING + [core] * (RING + 2)
    first, send, keep, own = pl.pallas_call(
        functools.partial(weight_kernel, counts),
        in_specs=[smem] + [vmem] * 5,
        out_specs=[hbm] * 4,
        out_shape=[shape((count,) + block, bf16) for count in counts],
        scratch_shapes=[pltpu.VMEM((2,) + block, bf16), pltpu.SemaphoreType.DMA((2,))],
        compiler_params=params(),
        name="partial",
    )(jnp.stack(tiles + flips), grads, saved, rstd, gains[0], right)
    summed = scatter_sum(keep, first, send, own, shards, core)
    weight_grad = (jnp.transpose(summed, (0, 2, 1)) / shards)[None]
    return (boundary[None], weight_grad)


def solution(mesh):
    return jax.shard_map(
        body,
        mesh=mesh,
        in_specs=(
            P(None, "fsdp", None),
            P("section", None, None, "fsdp", None),
            P("section", None, None, "fsdp", None),
            P("section", None, None, "fsdp", None),
            P(None, "fsdp", None),
            P("section", None, "fsdp", None),
            P("section", None, None),
        ),
        out_specs=(P("section", None, "fsdp", None), P("section", None, "fsdp", None)),
        check_vma=False,
    )
```

```python
import functools
import math

import jax
import jax.numpy as jnp
from jax import lax
from jax.experimental import pallas as pl
from jax.experimental.pallas import tpu as pltpu
from jax.sharding import PartitionSpec as P

HEADS = 4
HEAD_DIM = 128
EPS = 1e-05
CHUNK = 512
BLOCKS = 16
RING = 7
VMEM_LIMIT = 20 * 1024 * 1024
VMEM_VALUES = 56 * 1024 * 1024
VMEM_ALL = 62 * 1024 * 1024


def pre_kernel(x_ref, q_ref, k_ref, seg_row_ref, seg_col_ref, rstd_ref, probs_ref):
    length, width = x_ref.shape[2:]
    total = jnp.zeros((length, 1), jnp.float32)
    for at in range(0, width, CHUNK):
        part = x_ref[0, 0, :, at : at + CHUNK].astype(jnp.float32)
        total += jnp.sum(part * part, -1, keepdims=True)
    rstd = lax.rsqrt(total / width + EPS)
    rstd_ref[0, 0] = jnp.broadcast_to(rstd, (length, 128))
    rows = lax.broadcasted_iota(jnp.int32, (length, length), 0)
    columns = lax.broadcasted_iota(jnp.int32, (length, length), 1)
    allowed = (rows >= columns) & (seg_col_ref[0] == seg_row_ref[0])
    for head in range(HEADS):
        own = slice(head * HEAD_DIM, (head + 1) * HEAD_DIM)
        scores = lax.dot_general(
            q_ref[0, 0, :, own],
            k_ref[0, 0, :, own],
            (((1,), (1,)), ((), ())),
            preferred_element_type=jnp.float32,
        ) * (1.0 / math.sqrt(HEAD_DIM))
        scores = jnp.where(allowed, scores, -1e30)
        peak = jnp.max(scores, -1, keepdims=True)
        expo = jnp.where(allowed, jnp.exp(scores - peak), 0.0)
        probs = expo / jnp.sum(expo, -1, keepdims=True)
        probs_ref[0, 0, head] = probs.astype(jnp.bfloat16)


def value_kernel(place_ref, *refs):
    blocks, refs = refs[:BLOCKS], refs[BLOCKS:]
    saved, rstd, gains, probs, weight, vals, mixed, _, _, _, _, w_buf, x_buf, sems, x_sem, out_sem = refs
    batches, length, width = saved.shape[1:]
    rank = w_buf.shape[2]
    x_copies = [
        pltpu.make_async_copy(saved.at[layer], x_buf.at[layer], x_sem.at[layer]) for layer in (0, 1)
    ]
    loads = [[], []]
    rows = blocks[0].shape[2]
    for layer in (1, 0):
        for at, block in enumerate(blocks):
            for slot in (0, 1):
                start = pl.multiple_of(place_ref[2 * at + slot], rows)
                made = pltpu.make_async_copy(
                    block.at[slot, layer],
                    w_buf.at[layer, pl.ds(start, rows)],
                    sems.at[layer, 2 * at + slot],
                )
                made.start()
                loads[layer].append(made)
        x_copies[layer].start()
    stores = []
    for layer in (1, 0):
        for made in loads[layer]:
            made.wait()
        store = pltpu.make_async_copy(w_buf.at[layer], weight.at[layer], out_sem.at[layer])
        store.start()
        stores.append(store)
        x_copies[layer].wait()
        acc = jnp.zeros((batches * length, rank), jnp.float32)
        for at in range(0, width, CHUNK):
            cut = slice(at, at + CHUNK)
            gain = gains[layer : layer + 1, cut]
            normed = [
                (x_buf[layer, m, :, cut].astype(jnp.float32) * rstd[layer, m, :, 0:1] * gain)
                .astype(jnp.bfloat16)
                for m in range(batches)
            ]
            acc += jnp.dot(
                jnp.concatenate(normed, 0),
                w_buf[layer, cut, :],
                preferred_element_type=jnp.float32,
            )
        for m in range(batches):
            part = acc[m * length : (m + 1) * length]
            vals[layer, m] = part
            values = part.astype(jnp.bfloat16)
            for head in range(HEADS):
                own = slice(head * HEAD_DIM, (head + 1) * HEAD_DIM)
                mixed[layer, m, :, own] = jnp.dot(
                    probs[layer, m, head], values[:, own], preferred_element_type=jnp.float32
                ).astype(jnp.bfloat16)
    for store in stores:
        store.wait()


def tick_kernel(
    place_ref, incoming, upstream, saved, weight, gains, probs, vals, rstd,
    grads_in, dvs_in, boundary_in,
    out, grads, dvs, boundary,
    g_buf, x_buf, w_buf, gain_buf, p_buf, v_buf, r_buf, dv_buf, sems,
):
    del grads_in, dvs_in, boundary_in
    micro, top = place_ref[0], place_ref[1]
    batches = upstream.shape[0]
    width = incoming.shape[1]
    rank = weight.shape[2]
    count = width // CHUNK

    @pl.when((micro >= 0) & (micro < batches))
    def _():
        used = [0]

        def copy(source, target):
            made = pltpu.make_async_copy(source, target, sems.at[used[0]])
            used[0] += 1
            return made

        from_top = copy(upstream.at[micro], g_buf.at[0])
        from_above = pltpu.make_async_copy(incoming, g_buf.at[0], sems.at[used[0] - 1])

        @pl.when(top == 1)
        def _():
            from_top.start()

        @pl.when(top == 0)
        def _():
            from_above.start()

        load_w, load_x, load_p, load_v, load_r = ({}, {}, {}, {}, {})
        load_gain = copy(gains, gain_buf)
        for layer in (1, 0):
            for c in range(count):
                rows = pl.ds(c * CHUNK, CHUNK)
                load_w[layer, c] = copy(weight.at[layer, rows], w_buf.at[layer, rows])
            load_p[layer] = copy(probs.at[layer, micro], p_buf.at[layer])
            load_v[layer] = copy(vals.at[layer, micro], v_buf.at[layer])
            load_r[layer] = copy(rstd.at[layer, micro], r_buf.at[layer])
            load_x[layer] = copy(saved.at[layer, micro], x_buf.at[layer])
        for c in range(count):
            load_w[1, c].start()
        for made in (load_p[1], load_v[1], load_r[1], load_gain, load_x[1]):
            made.start()
        for c in range(count):
            load_w[0, c].start()
        for made in (load_p[0], load_v[0], load_r[0], load_x[0]):
            made.start()

        from_top.wait()
        acc = None
        for c in range(count):
            load_w[1, c].wait()
            rows = slice(c * CHUNK, (c + 1) * CHUNK)
            term = jnp.dot(
                g_buf[0, :, rows], w_buf[1, rows, :], preferred_element_type=jnp.float32
            )
            acc = term if acc is None else acc + term
        stores = [copy(g_buf.at[0], grads.at[1, micro])]
        stores[0].start()
        load_gain.wait()
        for step, layer in enumerate((1, 0)):
            dmix = acc.astype(jnp.bfloat16)
            load_p[layer].wait()
            for head in range(HEADS):
                own = slice(head * HEAD_DIM, (head + 1) * HEAD_DIM)
                dv_buf[layer, :, own] = lax.dot_general(
                    p_buf[layer, head],
                    dmix[:, own],
                    (((0,), (0,)), ((), ())),
                    preferred_element_type=jnp.float32,
                ).astype(jnp.bfloat16)
            stores.append(copy(dv_buf.at[layer], dvs.at[layer, micro]))
            stores[-1].start()
            dv = dv_buf[layer]
            load_v[layer].wait()
            load_r[layer].wait()
            scale = r_buf[layer, :, 0:1]
            mean = jnp.sum(dv.astype(jnp.float32) * v_buf[layer], -1, keepdims=True) / width
            pull = scale * scale * mean
            load_x[layer].wait()
            acc = None
            for c in range(count):
                rows = slice(c * CHUNK, (c + 1) * CHUNK)
                dnormed = lax.dot_general(
                    dv, w_buf[layer, rows, :], (((1,), (1,)), ((), ())),
                    preferred_element_type=jnp.float32,
                )
                lower = (
                    g_buf[step, :, rows].astype(jnp.float32)
                    + scale * (dnormed * gain_buf[layer : layer + 1, rows])
                    - x_buf[layer, :, rows].astype(jnp.float32) * pull
                ).astype(jnp.bfloat16)
                g_buf[step + 1, :, rows] = lower
                if layer == 1:
                    load_w[0, c].wait()
                    term = jnp.dot(
                        lower, w_buf[0, rows, :], preferred_element_type=jnp.float32
                    )
                    acc = term if acc is None else acc + term
                elif c % 2 == 1:
                    piece = pl.ds((c - 1) * CHUNK, 2 * CHUNK)
                    for target in (out.at[:, piece], boundary.at[micro, :, piece]):
                        stores.append(copy(g_buf.at[2, :, piece], target))
                        stores[-1].start()
            if layer == 1:
                stores.append(copy(g_buf.at[1], grads.at[0, micro]))
                stores[-1].start()
        for store in stores:
            store.wait()


def transpose_kernel(mixed_ref, dv_ref, right_ref):
    batches, length = mixed_ref.shape[1:3]
    rows = batches * length
    for layer in (0, 1):
        for m in range(batches):
            at = m * length
            right_ref[layer, :, at : at + length] = mixed_ref[layer, m].T
            right_ref[layer, :, rows + at : rows + at + length] = dv_ref[layer, m].T


def weight_kernel(counts, place_ref, g_ref, x_ref, rstd_ref, gain_ref, right_ref, *refs):
    outs, (buf, sems) = refs[: len(counts)], refs[len(counts) :]
    tiles = sum(counts)
    batches, length = g_ref.shape[1:3]
    wide = 2 * length

    def store(tile, slot, target, at):
        return pltpu.make_async_copy(buf.at[slot], target.at[at], sems.at[slot])

    def step(tile, carry):
        slot = lax.rem(tile, 2)
        start = pl.multiple_of(place_ref[tile] * wide, wide)
        cut = pl.ds(start, wide)

        @pl.when(tile >= 2)
        def _():
            store(tile, slot, outs[0], 0).wait()

        for layer in (0, 1):
            left = [g_ref[layer, m, :, cut] for m in range(batches)]
            left += [
                (
                    x_ref[layer, m, :, cut].astype(jnp.float32)
                    * rstd_ref[layer, m, :, 0:1]
                    * gain_ref[layer : layer + 1, cut]
                ).astype(jnp.bfloat16)
                for m in range(batches)
            ]
            result = jnp.dot(
                right_ref[layer], jnp.concatenate(left, 0), preferred_element_type=jnp.float32
            ).astype(jnp.bfloat16)
            turned = place_ref[tiles + tile]
            buf[slot, turned, layer] = result[:, :length]
            buf[slot, 1 - turned, layer] = result[:, length:]

        low = 0
        for count, out in zip(counts, outs):

            @pl.when((tile >= low) & (tile < low + count))
            def _(low=low, count=count, out=out):
                store(tile, slot, out, jnp.clip(tile - low, 0, count - 1)).start()

            low += count

        return carry

    lax.fori_loop(0, tiles, step, 0)
    for tile in (tiles - 2, tiles - 1):
        store(tile, tile % 2, outs[0], 0).wait()


def params(limit=VMEM_LIMIT):
    return pltpu.CompilerParams(vmem_limit_bytes=limit)


def other_core(value, shards):
    return lax.ppermute(value, "fsdp", [(d, d ^ 1) for d in range(shards)])


def other_y(value, shards):
    return lax.ppermute(value, "fsdp", [(d, d ^ 2) for d in range(shards)])


def along_z(value, shards):
    return lax.ppermute(
        value, "fsdp", [(d, (d + (4 if d % 2 == 0 else shards - 4)) % shards) for d in range(shards)]
    )


def gather_blocks(own_rows, shards, core, early):
    near = jnp.stack([own_rows, other_core(own_rows, shards)])
    rows_near = [near]
    far_rows = other_y(own_rows, shards)
    near = along_z(near, shards)
    near, far_rows = lax.optimization_barrier((near, far_rows))
    rows_near += [near, other_core(near, shards)]
    far = jnp.stack([far_rows, other_core(far_rows, shards)])
    rows_far = [far]
    for k in (1, 2, 3):
        if k == 2:
            far, early = lax.optimization_barrier((far, early))
        if k > 1:
            near = along_z(near, shards)
            rows_near += [near, other_core(near, shards)]
        far = along_z(far, shards)
        rows_far += [far, other_core(far, shards)]
    last = along_z(jnp.where(core == 0, near, far), shards)
    return rows_near + rows_far + [last, other_core(last, shards)], early


def wait_kernel(value_ref, word_ref, out_ref):
    del value_ref, word_ref, out_ref


def in_turn(value, pairs, shards):
    axes = ("section", "fsdp")

    def of_core(core):
        return [(a * shards + d, b * shards + d) for a, b in pairs for d in range(core, shards, 2)]

    lead = lax.ppermute(value, axes, of_core(0))
    word = lax.ppermute(
        lead[:8, :128], axes, [(a * shards + d, a * shards + d + 1) for a, _ in pairs for d in range(0, shards, 2)]
    )
    hbm = pl.BlockSpec(memory_space=pltpu.HBM)
    value = pl.pallas_call(
        wait_kernel,
        in_specs=[hbm, hbm],
        out_specs=hbm,
        out_shape=jax.ShapeDtypeStruct(value.shape, value.dtype),
        input_output_aliases={0: 0},
        compiler_params=params(),
        name="turn",
    )(value, word)
    return lead + lax.ppermute(value, axes, of_core(1))


def add_kernel(*refs):
    total = refs[0][...].astype(jnp.float32)
    for ref in refs[1:-1]:
        total += ref[...].astype(jnp.float32)
    refs[-1][...] = total.astype(jnp.bfloat16).reshape(refs[-1].shape)


def rounded_sum(*terms):
    block = terms[0][0].shape[1:]

    def spec(at):
        return pl.BlockSpec((1, 1) + block[1:], lambda i: (at, i) + (0,) * (len(block) - 1))

    return pl.pallas_call(
        add_kernel,
        grid=(block[0],),
        in_specs=[spec(at) for _, at in terms],
        out_specs=pl.BlockSpec((1,) + block[1:], lambda i: (i,) + (0,) * (len(block) - 1)),
        out_shape=jax.ShapeDtypeStruct(block, jnp.bfloat16),
        compiler_params=params(),
        name="plus",
    )(*[array for array, _ in terms])


def scatter_sum(keep, first, send, own, shards, core):
    taken_first = other_core(first, shards)
    taken = other_core(send, shards)
    came = along_z(rounded_sum((keep, 0), (taken_first, 0)), shards)
    zero = jnp.zeros_like(came)
    far = rounded_sum((keep, 2), (taken, 1), (jnp.where(core == 1, came, zero)[None], 0))
    near = rounded_sum((keep, 1), (taken, 0), (jnp.where(core == 0, came, zero)[None], 0))
    for k in (1, 2, 3):
        far = along_z(far, shards)
        near = along_z(near, shards)
        far = rounded_sum((far[None], 0), *([(keep, 2 * k + 2), (taken, 2 * k + 1)] if k < 3 else [(own, 1)]))
        near = rounded_sum((near[None], 0), *([(keep, 2 * k + 1), (taken, 2 * k)] if k < 3 else [(own, 0)]))
    far_own = far[0].astype(jnp.float32) + other_core(far[1], shards).astype(jnp.float32)
    far_own = other_y(far_own.astype(jnp.bfloat16), shards).astype(jnp.float32)
    near_own = near[0].astype(jnp.float32) + other_core(near[1], shards).astype(jnp.float32)
    return near_own + far_own


def body(upstream, saved_inputs, queries, keys, segments, weights, gains):
    sections = lax.axis_size("section")
    section_index = lax.axis_index("section")
    shards = lax.axis_size("fsdp")
    batches, length, width = upstream.shape
    rank = weights.shape[3]
    saved = saved_inputs[0]
    seg_row = segments
    seg_col = jnp.transpose(segments, (0, 2, 1))
    bf16, f32 = (jnp.bfloat16, jnp.float32)
    shape = jax.ShapeDtypeStruct
    any_spec = pl.BlockSpec(memory_space=pl.ANY)

    position = lax.axis_index("fsdp").astype(jnp.int32)
    z, y_hi, core = position // 4, position // 2 % 2, position % 2
    chips = shards // 4
    own_rows = weights[0]
    pair = lambda *tail: pl.BlockSpec((1, 1) + tail, lambda l, m: (l, m) + (0,) * len(tail))
    rstd, probs = pl.pallas_call(
        pre_kernel,
        grid=(2, batches),
        in_specs=[
            pair(length, width),
            pair(length, rank),
            pair(length, rank),
            pl.BlockSpec((1, 1, length), lambda l, m: (m, 0, 0)),
            pl.BlockSpec((1, length, 1), lambda l, m: (m, 0, 0)),
        ],
        out_specs=[pair(length, 128), pair(HEADS, length, length)],
        out_shape=[
            shape((2, batches, length, 128), f32),
            shape((2, batches, HEADS, length, length), bf16),
        ],
        compiler_params=params(),
        name="rows_alone",
    )(saved, queries[0], keys[0], seg_row, seg_col)

    gathered, (rstd, probs) = gather_blocks(own_rows, shards, core, (rstd, probs))

    turn = 1 - 2 * core
    starts = []

    def row_of(chip, high, low):
        return chip % chips * 4 * length + high * 2 * length + low * length

    for high in (y_hi, 1 - y_hi):
        starts += [row_of(z, high, core), row_of(z, high, 1 - core)]
        for k in (1, 2, 3):
            starts += [row_of(z - turn * k + chips, high, core), row_of(z - turn * k + chips, high, 1 - core)]
            starts += [row_of(z + turn * k + chips, high, 1 - core), row_of(z + turn * k + chips, high, core)]
    far = y_hi ^ core
    starts += [row_of(z + 4, far, core), row_of(z + 4, far, 1 - core)]
    starts += [row_of(z + 4, 1 - far, 1 - core), row_of(z + 4, 1 - far, core)]
    smem = pl.BlockSpec(memory_space=pltpu.SMEM)
    vmem = pl.BlockSpec(memory_space=pltpu.VMEM)
    hbm = pl.BlockSpec(memory_space=pltpu.HBM)
    grads_shape = shape((2, batches, length, width), bf16)
    dvs_shape = shape((2, batches, length, rank), bf16)
    boundary_shape = shape((batches, length, width), bf16)
    out_shape = shape((length, width), bf16)
    full_weight, vals, mixed, grads, dvs, boundary, incoming = pl.pallas_call(
        value_kernel,
        in_specs=[smem] + [hbm] * (BLOCKS + 1) + [vmem] * 3,
        out_specs=[hbm, vmem, vmem] + [hbm] * 4,
        out_shape=[
            shape((2, width, rank), bf16),
            shape((2, batches, length, rank), f32),
            shape((2, batches, length, rank), bf16),
            grads_shape,
            dvs_shape,
            boundary_shape,
            out_shape,
        ],
        scratch_shapes=[
            pltpu.VMEM((2, width, rank), bf16),
            pltpu.VMEM((2, batches, length, width), bf16),
            pltpu.SemaphoreType.DMA((2, 2 * BLOCKS)),
            pltpu.SemaphoreType.DMA((2,)),
            pltpu.SemaphoreType.DMA((2,)),
        ],
        compiler_params=params(VMEM_VALUES),
        name="values",
    )(jnp.stack(starts), *gathered, saved, rstd, gains[0], probs)

    tick = pl.pallas_call(
        tick_kernel,
        in_specs=[smem] + [hbm] * 11,
        out_specs=[hbm] * 4,
        out_shape=[out_shape, grads_shape, dvs_shape, boundary_shape],
        input_output_aliases={9: 1, 10: 2, 11: 3},
        scratch_shapes=[
            pltpu.VMEM((3, length, width), bf16),
            pltpu.VMEM((2, length, width), bf16),
            pltpu.VMEM((2, width, rank), bf16),
            pltpu.VMEM((2, width), f32),
            pltpu.VMEM((2, HEADS, length, length), bf16),
            pltpu.VMEM((2, length, rank), f32),
            pltpu.VMEM((2, length, 128), f32),
            pltpu.VMEM((2, length, rank), bf16),
            pltpu.SemaphoreType.DMA((48,)),
        ],
        compiler_params=params(VMEM_ALL),
        name="section",
    )

    top = (section_index == sections - 1).astype(jnp.int32)
    for step in range(sections + batches - 1):
        micro = step - (sections - 1 - section_index)
        place = jnp.stack([micro.astype(jnp.int32), top])
        out, grads, dvs, boundary = tick(
            place, incoming, upstream, saved, full_weight, gains[0], probs, vals, rstd,
            grads, dvs, boundary,
        )
        if step < sections + batches - 2:
            senders = [sections - 1 - step + m for m in range(batches)]
            pairs = [(s, s - 1) for s in senders if 1 <= s < sections]
            if step == 0:
                incoming = in_turn(out, pairs, shards)
            else:
                incoming = lax.ppermute(out, "section", pairs)

    def tiles_of(low):
        way = 1 - 2 * low
        tiles = [(z + 4) % chips * 2 + (y_hi ^ low)]
        for k in (3, 2, 1):
            for high in (y_hi, 1 - y_hi):
                tiles.append((z + way * k + chips) % chips * 2 + high)
        return tiles

    right = pl.pallas_call(
        transpose_kernel,
        in_specs=[vmem] * 2,
        out_specs=vmem,
        out_shape=shape((2, rank, 2 * batches * length), bf16),
        compiler_params=params(),
        name="factors",
    )(mixed, dvs)
    block = (2, 2, rank, length)

    counts = (1, RING - 1, RING, 2)
    tiles = tiles_of(1 - core) + tiles_of(core) + [z * 2 + y_hi, z * 2 + 1 - y_hi]
    flips = [1 - core] * RING + [core] * (RING + 2)
    first, send, keep, own = pl.pallas_call(
        functools.partial(weight_kernel, counts),
        in_specs=[smem] + [vmem] * 5,
        out_specs=[hbm] * 4,
        out_shape=[shape((count,) + block, bf16) for count in counts],
        scratch_shapes=[pltpu.VMEM((2,) + block, bf16), pltpu.SemaphoreType.DMA((2,))],
        compiler_params=params(),
        name="partial",
    )(jnp.stack(tiles + flips), grads, saved, rstd, gains[0], right)
    summed = scatter_sum(keep, first, send, own, shards, core)
    weight_grad = (jnp.transpose(summed, (0, 2, 1)) / shards)[None]
    return (boundary[None], weight_grad)


def solution(mesh):
    return jax.shard_map(
        body,
        mesh=mesh,
        in_specs=(
            P(None, "fsdp", None),
            P("section", None, None, "fsdp", None),
            P("section", None, None, "fsdp", None),
            P("section", None, None, "fsdp", None),
            P(None, "fsdp", None),
            P("section", None, "fsdp", None),
            P("section", None, None),
        ),
        out_specs=(P("section", None, "fsdp", None), P("section", None, "fsdp", None)),
        check_vma=False,
    )
```
